32 devices in a mesh: groups: 2 (over y), seq: 16 (over z, x, core).
Axes of the slice: x: 2, y: 2, z: 4, core: 2. Of those that a mesh axis runs over, the one named last changes fastest.
Arguments:
- queries: bfloat16 [32768, 512], P(('groups', 'seq')), parts along dimension 0, may hold values from -8 to 8
- video_keys: bfloat16 [32768, 512], P(('groups', 'seq')), parts along dimension 0, may hold values from -8 to 8
- video_values: bfloat16 [32768, 512], P(('groups', 'seq')), parts along dimension 0, may hold values from -6 to 6
- text_keys: bfloat16 [512, 512], P(('groups', 'seq')), parts along dimension 0, may hold values from -6 to 6
- text_values: bfloat16 [512, 512], P(('groups', 'seq')), parts along dimension 0, may hold values from -6 to 6
- block_lists: int32 [4, 256, 9], P(None, ('groups', 'seq')), parts along dimension 1, may hold values from 0 to 127, as said below
- list_lengths: int32 [4, 256], P(None, ('groups', 'seq')), parts along dimension 1, may hold values from 1 to 9, as said below
Outputs:
- attended: bfloat16 [32768, 512], P(('groups', 'seq')), parts along dimension 0
The draws below stay inside these ranges and needn't reach their ends.
There are 2 independent parts, one for each index of `groups`. The reference program is written for one: setup_inputs(seed, part) draws one part's arguments, and reference() takes and returns one part's arrays. A program takes and returns all parts, laid end to end along the dimension named above; each array names one. Nothing has to cross between parts.
Inputs may be any that keep to these rules, and one draw needn't show every extreme that they name: `block_lists`: the list of head h and query block a starts with a itself, followed by list_lengths[h, a] - 1 other distinct key blocks b with |b - a| <= 8; entries from position list_lengths[h, a] on equal a. `list_lengths`: some list is 9 long and some list is 1 long in every draw.
All inputs are finite; a program needn't handle non-finite values.
Results may differ from the reference program's by a relative error of at most 0.0055.
Values may be sent and summed in bfloat16 or wider, within the bound.
No kernel may reach another device: no remote copies, remote signals or barrier semaphores. Data moves between devices by JAX's collectives and lax.ppermute only.
A program may use at most 64 MiB of HBM per device.

```python
import jax
import jax.numpy as jnp
from jax import lax

HEAD_DIM = 128
HEADS = 4
BLOCK = 128
REACH = 8
MAXLEN = 9
TEXT = 256
SEQ_LEN = 16384


def draw_queries(key, part):
    key = jax.random.fold_in(key, 5)
    return jnp.clip(jax.random.normal(key, (SEQ_LEN, HEADS * HEAD_DIM), jnp.float32), -6.0, 6.0).astype(jnp.bfloat16)


def draw_video_keys(key, part):
    key = jax.random.fold_in(key, 6)
    return jnp.clip(jax.random.normal(key, (SEQ_LEN, HEADS * HEAD_DIM), jnp.float32), -6.0, 6.0).astype(jnp.bfloat16)


def lengths_drawn(key):
    block_count = SEQ_LEN // BLOCK
    level_key, head_key, count_key, top_key, bottom_key = jax.random.split(key, 5)
    regions = (block_count + 7) // 8
    level = jax.random.randint(level_key, (regions,), 2, 5)
    level_rows = jnp.repeat(level, 8)[:block_count]
    head_scale = jax.random.randint(head_key, (HEADS,), 2, 5)
    ceiling = jnp.maximum(1, MAXLEN * level_rows[None, :] * head_scale[:, None] // 16)
    counts = ceiling - jax.random.randint(count_key, (HEADS, block_count), 0, (ceiling + 1) // 2)
    top_at = jax.random.randint(top_key, (), 0, block_count)
    bottom_at = jax.random.randint(bottom_key, (), 0, block_count)
    counts = counts.at[0, top_at].set(MAXLEN)
    counts = counts.at[1, bottom_at].set(1)
    return counts.astype(jnp.int32)


def draw_list_lengths(key, part):
    counts = lengths_drawn(key)
    return counts


def draw_block_lists(key, part):
    counts = lengths_drawn(key)
    key = jax.random.fold_in(key, 9)
    block_count = SEQ_LEN // BLOCK
    offsets = jnp.concatenate([jnp.arange(-REACH, 0, dtype=jnp.int32), jnp.arange(1, REACH + 1, dtype=jnp.int32)])
    noise = jax.random.randint(key, (HEADS, block_count, 2 * REACH), 0, 1 << 20)
    target = jnp.arange(block_count, dtype=jnp.int32)[None, :, None] + offsets[None, None, :]
    outside = ((target < 0) | (target >= block_count)).astype(jnp.int32)
    ranking = noise * (2 * REACH) + jnp.arange(2 * REACH, dtype=jnp.int32) + outside * (1 << 26)
    ranked = jnp.argsort(ranking, axis=-1)
    chosen = jnp.take_along_axis(target, ranked, axis=-1)[:, :, :MAXLEN - 1]
    own_block = jnp.broadcast_to(jnp.arange(block_count, dtype=jnp.int32)[None, :, None], (HEADS, block_count, 1))
    filled = jnp.concatenate([own_block, chosen], axis=-1)
    live = jnp.arange(MAXLEN, dtype=jnp.int32)[None, None, :] < counts[:, :, None]
    return jnp.where(live, filled, own_block).astype(jnp.int32)


def level_of(own_key, extent, shards, smallest, top_value):
    def one(dim, blocks):
        heights = jax.random.uniform(jax.random.fold_in(jax.random.fold_in(own_key, 6), dim), (blocks,), jnp.float32, smallest / len(shards), top_value / len(shards))
        return jnp.repeat(jnp.exp(heights), extent[dim] // blocks).reshape((-1,) + (1,) * (len(extent) - dim - 1))

    loudness = one(*shards[0])
    for cut in shards[1:]:
        loudness = loudness * one(*cut)
    return loudness


def normal_values(own_key, dims, deviation, reach, shards=(), kind=jnp.bfloat16):
    array = deviation * jax.random.normal(own_key, dims, jnp.float32)
    if shards:
        array = array * level_of(own_key, dims, shards, -0.22, 0.18)
    return jnp.clip(array, -reach, reach).astype(kind)


def setup_inputs(seed: int = 0, part: int = 0) -> dict:
    streams_of = jax.random.split(jax.random.key(seed), 8)
    part_keys = jax.random.split(jax.random.fold_in(streams_of[7], part), 8)
    return {
        "queries": draw_queries(jax.random.fold_in(jax.random.fold_in(streams_of[7], part), 71), part),
        "video_keys": draw_video_keys(jax.random.fold_in(jax.random.fold_in(streams_of[7], part), 71), part),
        "video_values": normal_values(part_keys[2], (SEQ_LEN, HEADS * HEAD_DIM), 1.0, 6.0, ((0, 16),)),
        "text_keys": normal_values(part_keys[3], (TEXT, HEADS * HEAD_DIM), 1.0, 6.0, ((0, 16),)),
        "text_values": normal_values(part_keys[4], (TEXT, HEADS * HEAD_DIM), 1.0, 6.0, ((0, 16),)),
        "block_lists": draw_block_lists(jax.random.fold_in(jax.random.fold_in(streams_of[7], part), 71), part),
        "list_lengths": draw_list_lengths(jax.random.fold_in(jax.random.fold_in(streams_of[7], part), 71), part),
    }


def reference(queries, video_keys, video_values, text_keys, text_values, block_lists, list_lengths):
    block_count = SEQ_LEN // BLOCK
    score_scale = HEAD_DIM ** -0.5
    query_tiles = queries.reshape(block_count, BLOCK, HEADS, HEAD_DIM)
    key_tiles = video_keys.reshape(block_count, BLOCK, HEADS, HEAD_DIM)
    value_tiles = video_values.reshape(block_count, BLOCK, HEADS, HEAD_DIM)
    text_key_heads = text_keys.reshape(TEXT, HEADS, HEAD_DIM)
    text_value_heads = text_values.reshape(TEXT, HEADS, HEAD_DIM)
    live_rows = jnp.arange(MAXLEN * BLOCK, dtype=jnp.int32) // BLOCK

    def one_unit(unit_index):
        head_index = unit_index // block_count
        block_index = unit_index % block_count
        query_block = lax.dynamic_index_in_dim(query_tiles, block_index, 0, False)
        query_rows = lax.dynamic_index_in_dim(query_block, head_index, 1, False)
        entries = block_lists[head_index, block_index]
        live_count = list_lengths[head_index, block_index]
        picked_keys = lax.dynamic_index_in_dim(jnp.take(key_tiles, entries, axis=0), head_index, 2, False)
        picked_values = lax.dynamic_index_in_dim(jnp.take(value_tiles, entries, axis=0), head_index, 2, False)
        all_keys = jnp.concatenate([lax.dynamic_index_in_dim(text_key_heads, head_index, 1, False),
                                    picked_keys.reshape(MAXLEN * BLOCK, HEAD_DIM)], axis=0)
        all_values = jnp.concatenate([lax.dynamic_index_in_dim(text_value_heads, head_index, 1, False),
                                      picked_values.reshape(MAXLEN * BLOCK, HEAD_DIM)], axis=0)
        valid = jnp.concatenate([jnp.ones((TEXT,), dtype=bool), live_rows < live_count])
        scores = jnp.dot(query_rows, all_keys.T, preferred_element_type=jnp.float32) * score_scale
        scores = jnp.where(valid[None, :], scores, -jnp.inf)
        row_top = jnp.max(scores, axis=1, keepdims=True)
        weights = jnp.exp(scores - row_top)
        row_total = jnp.sum(weights, axis=1, keepdims=True)
        summed = jnp.dot(weights.astype(jnp.bfloat16), all_values, preferred_element_type=jnp.float32)
        return (summed / row_total).astype(jnp.bfloat16)

    results = lax.map(one_unit, jnp.arange(HEADS * block_count, dtype=jnp.int32))
    merged = results.reshape(HEADS, block_count, BLOCK, HEAD_DIM).transpose(1, 2, 0, 3)
    return merged.reshape(SEQ_LEN, HEADS * HEAD_DIM)
```

```python
import functools
import math

import jax
import jax.numpy as jnp
from jax import lax
from jax.experimental import pallas as pl
from jax.experimental.pallas import tpu as pltpu
from jax.sharding import PartitionSpec as P

HEAD_DIM = 128
HEADS = 4
BLOCK = 128
REACH = 8
GROUP = 4
EXP2_SCALE = HEAD_DIM ** (-0.5) * math.log2(math.e)
NEVER = -1e30
NT = (((1,), (1,)), ((), ()))
VMEM_BYTES = 40 * 1024 * 1024


def aligned(index):
    return pl.ds(pl.multiple_of(index * BLOCK, BLOCK), BLOCK)


def partial_attention(keys, query_rows, values_t):
    scores = lax.dot_general(keys, query_rows, NT, preferred_element_type=jnp.float32)
    top = jnp.max(scores, axis=0, keepdims=True)
    weights = jnp.exp2((scores - top) * EXP2_SCALE)
    total = jnp.sum(weights, axis=0, keepdims=True)
    summed = jnp.dot(values_t, weights.astype(jnp.bfloat16), preferred_element_type=jnp.float32)
    return top, total, summed


def merge(unit, part, tops, totals, sums):
    top, total, summed = part
    old_top = tops[unit]
    new_top = jnp.maximum(old_top, top)
    keep = jnp.exp2((old_top - new_top) * EXP2_SCALE)
    add = jnp.exp2((top - new_top) * EXP2_SCALE)
    tops[unit] = new_top
    totals[unit] = totals[unit] * keep + total * add
    sums[unit] = sums[unit] * keep + summed * add


def run_items(items, count, blocks_dev, q_ref, k_ref, vt_ref, tops, totals, sums):
    def step(group, carry):
        parts = []
        for slot in range(GROUP):
            position = group * GROUP + slot
            code = items[jnp.minimum(position, count - 1)]
            unit = code // 64
            block = code % 64
            head = unit // blocks_dev
            local = unit % blocks_dev
            top, total, summed = partial_attention(
                k_ref[aligned(block), aligned(head)],
                q_ref[aligned(local), aligned(head)],
                vt_ref[aligned(head), aligned(block)],
            )
            top = jnp.where(position < count, top, NEVER)
            parts.append((unit, (top, total, summed)))
        for unit, part in parts:
            merge(unit, part, tops, totals, sums)
        return carry

    lax.fori_loop(0, (count + GROUP - 1) // GROUP, step, 0)


def near_kernel(
    blocks_dev,
    longest,
    lists,
    lengths,
    q_ref,
    k_ref,
    vt_ref,
    text_k,
    text_v,
    tops,
    totals,
    sums,
    far_items,
    far_counts,
    own_items,
):
    base = lists[0]
    room = far_items.shape[1]

    def plan_unit(unit, counts):
        def plan_entry(entry, counts):
            own, low, high = counts
            block = lists[unit * longest + entry] - base
            code = unit * 64
            is_low = block < 0
            is_high = block >= blocks_dev
            is_own = jnp.logical_not(is_low | is_high)

            @pl.when(is_own)
            def _():
                own_items[own] = code + block

            @pl.when(is_low)
            def _():
                far_items[0, low] = code + block + blocks_dev

            @pl.when(is_high)
            def _():
                far_items[1, high] = code + block - blocks_dev

            return (
                own + is_own.astype(jnp.int32),
                low + is_low.astype(jnp.int32),
                high + is_high.astype(jnp.int32),
            )

        return lax.fori_loop(0, lengths[unit], plan_entry, counts)

    zero = jnp.int32(0)
    own, low, high = lax.fori_loop(0, HEADS * blocks_dev, plan_unit, (zero, zero, zero))
    far_counts[0] = low
    far_counts[1] = high

    def text_head(head, carry):
        keys = text_k[:, aligned(head)]
        values_t = text_v[:, aligned(head)].T
        for pair in range(blocks_dev // 2):
            rows = pl.ds(pair * 2 * BLOCK, 2 * BLOCK)
            top, total, summed = partial_attention(keys, q_ref[rows, aligned(head)], values_t)
            for side in range(2):
                unit = head * blocks_dev + pair * 2 + side
                lanes = slice(side * BLOCK, (side + 1) * BLOCK)
                tops[unit] = top[:, lanes]
                totals[unit] = total[:, lanes]
                sums[unit] = summed[:, lanes]
        return carry

    lax.fori_loop(0, HEADS, text_head, 0)
    run_items(own_items, own, blocks_dev, q_ref, k_ref, vt_ref, tops, totals, sums)


def far_kernel(
    blocks_dev,
    far_items,
    far_counts,
    q_ref,
    k_low,
    k_high,
    vt_low,
    vt_high,
    tops_in,
    totals_in,
    sums_in,
    out_ref,
    tops,
    totals,
    sums,
):
    tops[...] = tops_in[...]
    totals[...] = totals_in[...]
    sums[...] = sums_in[...]
    run_items(
        far_items.at[0], far_counts[0], blocks_dev, q_ref, k_low, vt_low, tops, totals, sums
    )
    run_items(
        far_items.at[1], far_counts[1], blocks_dev, q_ref, k_high, vt_high, tops, totals, sums
    )

    def finish(local, carry):
        for head in range(HEADS):
            unit = head * blocks_dev + local
            result = (sums[unit] / totals[unit]).T
            out_ref[aligned(local), head * HEAD_DIM : (head + 1) * HEAD_DIM] = result.astype(
                jnp.bfloat16
            )
        return carry

    lax.fori_loop(0, blocks_dev, finish, 0)


def on_device(queries, video_keys, video_values, text_keys, text_values, block_lists, list_lengths):
    tokens = queries.shape[0]
    blocks_dev = tokens // BLOCK
    assert blocks_dev >= REACH and blocks_dev % 2 == 0 and blocks_dev <= 64
    units = HEADS * blocks_dev
    longest = block_lists.shape[2]
    count = lax.axis_size("seq")
    forward = [(i, i + 1) for i in range(count - 1)]
    backward = [(target, source) for source, target in forward]

    values_t = video_values.T
    k_low = lax.ppermute(video_keys, "seq", forward)
    k_high = lax.ppermute(video_keys, "seq", backward)
    vt_low = lax.ppermute(values_t, "seq", forward)
    vt_high = lax.ppermute(values_t, "seq", backward)
    text_pair = lax.all_gather(jnp.stack([text_keys, text_values], 0), "seq", axis=1, tiled=True)

    lists = block_lists.reshape(units * longest)
    lengths = list_lengths.reshape(units)
    smem = pl.BlockSpec(memory_space=pltpu.SMEM)
    vmem = pl.BlockSpec(memory_space=pltpu.VMEM)
    stat = jax.ShapeDtypeStruct((units, 1, BLOCK), jnp.float32)
    total_sums = jax.ShapeDtypeStruct((units, HEAD_DIM, BLOCK), jnp.float32)
    room = units * longest
    tops, totals, sums, far_items, far_counts = pl.pallas_call(
        functools.partial(near_kernel, blocks_dev, longest),
        out_shape=(
            stat,
            stat,
            total_sums,
            jax.ShapeDtypeStruct((2, room), jnp.int32),
            jax.ShapeDtypeStruct((2,), jnp.int32),
        ),
        in_specs=[smem, smem] + [vmem] * 5,
        out_specs=(vmem, vmem, vmem, smem, smem),
        scratch_shapes=[pltpu.SMEM((room,), jnp.int32)],
        compiler_params=pltpu.CompilerParams(vmem_limit_bytes=VMEM_BYTES),
        cost_estimate=pl.CostEstimate(
            flops=1_500_000_000, bytes_accessed=8_000_000, transcendentals=4_000_000
        ),
        name="near",
    )(lists, lengths, queries, video_keys, values_t, text_pair[0], text_pair[1])
    return pl.pallas_call(
        functools.partial(far_kernel, blocks_dev),
        out_shape=jax.ShapeDtypeStruct((tokens, HEADS * HEAD_DIM), jnp.bfloat16),
        in_specs=[smem, smem] + [vmem] * 8,
        out_specs=vmem,
        scratch_shapes=[
            pltpu.VMEM((units, 1, BLOCK), jnp.float32),
            pltpu.VMEM((units, 1, BLOCK), jnp.float32),
            pltpu.VMEM((units, HEAD_DIM, BLOCK), jnp.float32),
        ],
        compiler_params=pltpu.CompilerParams(vmem_limit_bytes=VMEM_BYTES),
        cost_estimate=pl.CostEstimate(
            flops=1_000_000_000, bytes_accessed=9_000_000, transcendentals=2_000_000
        ),
        name="far",
    )(far_items, far_counts, queries, k_low, k_high, vt_low, vt_high, tops, totals, sums)


def solution(mesh):
    in_specs = (
        P(("groups", "seq"), None),
        P(("groups", "seq"), None),
        P(("groups", "seq"), None),
        P(("groups", "seq"), None),
        P(("groups", "seq"), None),
        P(None, ("groups", "seq"), None),
        P(None, ("groups", "seq")),
    )
    out_specs = P(("groups", "seq"), None)
    return jax.shard_map(
        on_device, mesh=mesh, in_specs=in_specs, out_specs=out_specs, check_vma=False
    )
```

```python
import functools
import math

import jax
import jax.numpy as jnp
from jax import lax
from jax.experimental import pallas as pl
from jax.experimental.pallas import tpu as pltpu
from jax.sharding import PartitionSpec as P

HEAD_DIM = 128
HEADS = 4
BLOCK = 128
REACH = 8
GROUP = 8
EXP2_SCALE = HEAD_DIM ** (-0.5) * math.log2(math.e)
NEVER = -1e30
NT = (((1,), (1,)), ((), ()))
VMEM_BYTES = 32 * 1024 * 1024
CODE = 64


def aligned(index):
    return pl.ds(pl.multiple_of(index * BLOCK, BLOCK), BLOCK)


def score_tile(keys, query_rows):
    return lax.dot_general(keys, query_rows, NT, preferred_element_type=jnp.float32)


def partial_attention(keys, query_rows, values_t):
    scores = score_tile(keys, query_rows)
    top = jnp.max(scores, axis=0, keepdims=True)
    weights = jnp.exp2((scores - top) * EXP2_SCALE)
    total = jnp.sum(weights, axis=0, keepdims=True)
    summed = jnp.dot(values_t, weights.astype(jnp.bfloat16), preferred_element_type=jnp.float32)
    return top, total, summed


def merge(unit, part, tops, totals, sums):
    top, total, summed = part
    old_top = tops[unit]
    new_top = jnp.maximum(old_top, top)
    keep = jnp.exp2((old_top - new_top) * EXP2_SCALE)
    add = jnp.exp2((top - new_top) * EXP2_SCALE)
    tops[unit] = new_top
    totals[unit] = totals[unit] * keep + total * add
    sums[unit] = sums[unit] * keep + summed * add


def for_groups(count, items, blocks_dev, body):
    def step(group, carry):
        slots = []
        for slot in range(GROUP):
            position = group * GROUP + slot
            code = items[jnp.minimum(position, count - 1)]
            unit = code // CODE
            slots.append(
                (
                    position,
                    position < count,
                    unit,
                    unit // blocks_dev,
                    unit % blocks_dev,
                    code % CODE,
                )
            )
        body(slots)
        return carry

    lax.fori_loop(0, (count + GROUP - 1) // GROUP, step, 0)


def own_kernel(
    blocks_dev,
    longest,
    lists,
    lengths,
    q_ref,
    k_ref,
    v_ref,
    tops,
    totals,
    sums,
    far_items,
    far_count,
    own_items,
    vt_ref,
):
    base = lists[0]

    def plan_unit(unit, counts):
        def plan_entry(entry, counts):
            own, far = counts
            block = lists[unit * longest + entry] - base
            code = unit * CODE
            is_own = jnp.logical_and(block >= 0, block < blocks_dev)

            @pl.when(is_own)
            def _():
                own_items[own] = code + block

            @pl.when(jnp.logical_not(is_own))
            def _():
                far_items[far] = code + jnp.where(block < 0, block + blocks_dev, block)

            mine = is_own.astype(jnp.int32)
            return own + mine, far + 1 - mine

        return lax.fori_loop(0, lengths[unit], plan_entry, counts)

    zero = jnp.int32(0)
    own, far = lax.fori_loop(0, HEADS * blocks_dev, plan_unit, (zero, zero))
    far_count[0] = far

    def turn(block, carry):
        for head in range(HEADS):
            lanes = slice(head * HEAD_DIM, (head + 1) * HEAD_DIM)
            vt_ref[lanes, aligned(block)] = v_ref[aligned(block), lanes].T
        return carry

    lax.fori_loop(0, blocks_dev, turn, 0)
    tops[...] = jnp.full(tops.shape, NEVER, jnp.float32)
    totals[...] = jnp.zeros(totals.shape, jnp.float32)
    sums[...] = jnp.zeros(sums.shape, jnp.float32)

    def body(slots):
        parts = []
        for position, live, unit, head, local, block in slots:
            top, total, summed = partial_attention(
                k_ref[aligned(block), aligned(head)],
                q_ref[aligned(local), aligned(head)],
                vt_ref[aligned(head), aligned(block)],
            )
            parts.append((unit, (jnp.where(live, top, NEVER), total, summed)))
        for unit, part in parts:
            merge(unit, part, tops, totals, sums)

    for_groups(own, own_items, blocks_dev, body)


def middle_kernel(
    blocks_dev,
    far_items,
    far_count,
    q_ref,
    k_low,
    k_high,
    text,
    tops_in,
    totals_in,
    sums_in,
    near_out,
    weights_out,
    k_far,
    tops,
    totals,
    sums,
    near_tops,
    levels,
    weights_all,
    sems,
    out_sems,
):
    tokens = k_low.shape[0]
    copies = [
        pltpu.make_async_copy(k_low, k_far.at[pl.ds(0, tokens)], sems.at[0]),
        pltpu.make_async_copy(k_high, k_far.at[pl.ds(tokens, tokens)], sems.at[1]),
    ]
    for copy in copies:
        copy.start()
    tops[...] = tops_in[...]
    totals[...] = totals_in[...]
    sums[...] = sums_in[...]

    def text_head(head, carry):
        keys = text[0, :, aligned(head)]
        values_t = text[1, :, aligned(head)].T
        for pair in range(blocks_dev // 2):
            rows = pl.ds(pair * 2 * BLOCK, 2 * BLOCK)
            top, total, summed = partial_attention(keys, q_ref[rows, aligned(head)], values_t)
            for side in range(2):
                unit = head * blocks_dev + pair * 2 + side
                lanes = slice(side * BLOCK, (side + 1) * BLOCK)
                merge(unit, (top[:, lanes], total[:, lanes], summed[:, lanes]), tops, totals, sums)
        return carry

    lax.fori_loop(0, HEADS, text_head, 0)
    for copy in copies:
        copy.wait()
    near_tops[...] = tops[...]
    count = far_count[0]

    def total_body(slots):
        found = []
        for position, live, unit, head, local, block in slots:
            scores = score_tile(
                k_far[aligned(block), aligned(head)], q_ref[aligned(local), aligned(head)]
            )
            top = jnp.max(scores, axis=0, keepdims=True)
            total = jnp.sum(jnp.exp2((scores - top) * EXP2_SCALE), axis=0, keepdims=True)
            found.append((unit, jnp.where(live, top, NEVER), total))
        for unit, top, total in found:
            old_top = tops[unit]
            new_top = jnp.maximum(old_top, top)
            tops[unit] = new_top
            totals[unit] = totals[unit] * jnp.exp2(
                (old_top - new_top) * EXP2_SCALE
            ) + total * jnp.exp2((top - new_top) * EXP2_SCALE)

    for_groups(count, far_items, blocks_dev, total_body)
    levels[...] = tops[...] * EXP2_SCALE + jnp.log2(totals[...])

    def weights_body(slots):
        for position, live, unit, head, local, block in slots:
            scores = score_tile(
                k_far[aligned(block), aligned(head)], q_ref[aligned(local), aligned(head)]
            )
            level = jnp.where(live, levels[unit], -NEVER)
            weights = jnp.exp2(scores * EXP2_SCALE - level).astype(jnp.bfloat16)
            weights_all[position] = weights.T
        first = pl.multiple_of(slots[0][0], GROUP)
        part = pl.ds(first, GROUP)
        pltpu.make_async_copy(
            weights_all.at[part], weights_out.at[part], out_sems.at[first // GROUP]
        ).start()

    for_groups(count, far_items, blocks_dev, weights_body)

    def near_rows(local, carry):
        for head in range(HEADS):
            unit = head * blocks_dev + local
            factor = jnp.exp2(near_tops[unit] * EXP2_SCALE - levels[unit])
            near_out[aligned(local), head * HEAD_DIM : (head + 1) * HEAD_DIM] = (
                sums[unit] * factor
            ).T
        return carry

    lax.fori_loop(0, blocks_dev, near_rows, 0)

    def settle(group, carry):
        part = pl.ds(pl.multiple_of(group * GROUP, GROUP), GROUP)
        pltpu.make_async_copy(weights_all.at[part], weights_out.at[part], out_sems.at[group]).wait()
        return carry

    lax.fori_loop(0, (count + GROUP - 1) // GROUP, settle, 0)


def last_kernel(
    blocks_dev,
    far_items,
    far_count,
    near,
    weights,
    v_low,
    v_high,
    out_ref,
    v_far,
    total_rows,
    weights_all,
    sems,
    weight_sems,
):
    tokens = v_low.shape[0]
    count = far_count[0]
    groups = (count + GROUP - 1) // GROUP

    def weight_copy(group):
        part = pl.ds(pl.multiple_of(group * GROUP, GROUP), GROUP)
        return pltpu.make_async_copy(weights.at[part], weights_all.at[part], weight_sems.at[group])

    copies = [
        pltpu.make_async_copy(v_low, v_far.at[pl.ds(0, tokens)], sems.at[0]),
        pltpu.make_async_copy(v_high, v_far.at[pl.ds(tokens, tokens)], sems.at[1]),
        pltpu.make_async_copy(near, total_rows, sems.at[2]),
    ]
    for copy in copies:
        copy.start()

    def begin(group, carry):
        weight_copy(group).start()
        return carry

    lax.fori_loop(0, groups, begin, 0)
    for copy in copies:
        copy.wait()

    def body(slots):
        weight_copy(slots[0][0] // GROUP).wait()
        parts = []
        for position, live, unit, head, local, block in slots:
            parts.append(
                jnp.dot(
                    weights_all[position],
                    v_far[aligned(block), aligned(head)],
                    preferred_element_type=jnp.float32,
                )
            )
        for slot, part in zip(slots, parts):
            total_rows[aligned(slot[4]), aligned(slot[3])] += part

    for_groups(count, far_items, blocks_dev, body)
    out_ref[...] = total_rows[...].astype(jnp.bfloat16)


def text_step(text, distance):
    count = lax.axis_size("seq")
    pairs = [(i, i ^ distance) for i in range(count)]
    return jnp.concatenate([text, lax.ppermute(text, "seq", pairs)], axis=1)


def on_device(queries, video_keys, video_values, text_keys, text_values, block_lists, list_lengths):
    tokens = queries.shape[0]
    columns = queries.shape[1]
    blocks_dev = tokens // BLOCK
    count = lax.axis_size("seq")
    assert blocks_dev == REACH and 2 * blocks_dev <= CODE and count & (count - 1) == 0
    units = HEADS * blocks_dev
    longest = block_lists.shape[2]
    forward = [(i, i + 1) for i in range(count - 1)]
    backward = [(target, source) for source, target in forward]

    k_low = lax.ppermute(video_keys, "seq", forward)
    k_high = lax.ppermute(video_keys, "seq", backward)
    text = text_step(jnp.stack([text_keys, text_values], 0), 2)
    v_low = lax.ppermute(video_values, "seq", forward)
    v_high = lax.ppermute(video_values, "seq", backward)
    distance = 4
    while distance < count:
        text = text_step(text, distance)
        distance *= 2
    text = text_step(text, 1)

    lists = block_lists.reshape(units * longest)
    lengths = list_lengths.reshape(units)
    smem = pl.BlockSpec(memory_space=pltpu.SMEM)
    vmem = pl.BlockSpec(memory_space=pltpu.VMEM)
    anywhere = pl.BlockSpec(memory_space=pl.ANY)
    stat = (units, 1, BLOCK)
    squares = (units, HEAD_DIM, BLOCK)
    room = -(-units * (longest - 1) // GROUP) * GROUP
    weights_shape = (room, BLOCK, BLOCK)
    params = pltpu.CompilerParams(vmem_limit_bytes=VMEM_BYTES)

    tops, totals, sums, far_items, far_count = pl.pallas_call(
        functools.partial(own_kernel, blocks_dev, longest),
        out_shape=(
            jax.ShapeDtypeStruct(stat, jnp.float32),
            jax.ShapeDtypeStruct(stat, jnp.float32),
            jax.ShapeDtypeStruct(squares, jnp.float32),
            jax.ShapeDtypeStruct((room,), jnp.int32),
            jax.ShapeDtypeStruct((1,), jnp.int32),
        ),
        in_specs=[smem, smem] + [vmem] * 3,
        out_specs=(vmem, vmem, vmem, smem, smem),
        scratch_shapes=[
            pltpu.SMEM((units * longest,), jnp.int32),
            pltpu.VMEM((columns, tokens), jnp.bfloat16),
        ],
        compiler_params=params,
        cost_estimate=pl.CostEstimate(
            flops=6_000_000_000, bytes_accessed=6_000_000, transcendentals=2_000_000
        ),
        name="own",
    )(lists, lengths, queries, video_keys, video_values)

    near, weights = pl.pallas_call(
        functools.partial(middle_kernel, blocks_dev),
        out_shape=(
            jax.ShapeDtypeStruct((tokens, columns), jnp.float32),
            jax.ShapeDtypeStruct(weights_shape, jnp.bfloat16),
        ),
        in_specs=[smem, smem, vmem, anywhere, anywhere] + [vmem] * 4,
        out_specs=(vmem, anywhere),
        scratch_shapes=[
            pltpu.VMEM((2 * tokens, columns), jnp.bfloat16),
            pltpu.VMEM(stat, jnp.float32),
            pltpu.VMEM(stat, jnp.float32),
            pltpu.VMEM(squares, jnp.float32),
            pltpu.VMEM(stat, jnp.float32),
            pltpu.VMEM(stat, jnp.float32),
            pltpu.VMEM(weights_shape, jnp.bfloat16),
            pltpu.SemaphoreType.DMA((2,)),
            pltpu.SemaphoreType.DMA((room // GROUP,)),
        ],
        compiler_params=params,
        cost_estimate=pl.CostEstimate(
            flops=8_000_000_000, bytes_accessed=12_000_000, transcendentals=5_000_000
        ),
        name="middle",
    )(far_items, far_count, queries, k_low, k_high, text, tops, totals, sums)

    return pl.pallas_call(
        functools.partial(last_kernel, blocks_dev),
        out_shape=jax.ShapeDtypeStruct((tokens, columns), jnp.bfloat16),
        in_specs=[smem, smem] + [anywhere] * 4,
        out_specs=vmem,
        scratch_shapes=[
            pltpu.VMEM((2 * tokens, columns), jnp.bfloat16),
            pltpu.VMEM((tokens, columns), jnp.float32),
            pltpu.VMEM(weights_shape, jnp.bfloat16),
            pltpu.SemaphoreType.DMA((3,)),
            pltpu.SemaphoreType.DMA((room // GROUP,)),
        ],
        compiler_params=params,
        cost_estimate=pl.CostEstimate(
            flops=1_000_000_000, bytes_accessed=9_000_000, transcendentals=0
        ),
        name="last",
    )(far_items, far_count, near, weights, v_low, v_high)


def solution(mesh):
    in_specs = (
        P(("groups", "seq"), None),
        P(("groups", "seq"), None),
        P(("groups", "seq"), None),
        P(("groups", "seq"), None),
        P(("groups", "seq"), None),
        P(None, ("groups", "seq"), None),
        P(None, ("groups", "seq")),
    )
    out_specs = P(("groups", "seq"), None)
    return jax.shard_map(
        on_device, mesh=mesh, in_specs=in_specs, out_specs=out_specs, check_vma=False
    )
```

```python
import functools
import math

import jax
import jax.numpy as jnp
from jax import lax
from jax.experimental import pallas as pl
from jax.experimental.pallas import tpu as pltpu
from jax.sharding import PartitionSpec as P

HEAD_DIM = 128
HEADS = 4
BLOCK = 128
REACH = 8
GROUP = 16
EXP2_SCALE = HEAD_DIM ** (-0.5) * math.log2(math.e)
NEVER = -1e30
NT = (((1,), (1,)), ((), ()))
VMEM_BYTES = 60 * 1024 * 1024
CODE = 64


def aligned(index):
    return pl.ds(pl.multiple_of(index * BLOCK, BLOCK), BLOCK)


def score_tile(keys, query_rows):
    return lax.dot_general(keys, query_rows, NT, preferred_element_type=jnp.float32)


def partial_attention(keys, query_rows, values_t):
    scores = score_tile(keys, query_rows)
    top = jnp.max(scores, axis=0, keepdims=True)
    weights = jnp.exp2((scores - top) * EXP2_SCALE)
    total = jnp.sum(weights, axis=0, keepdims=True)
    summed = jnp.dot(values_t, weights.astype(jnp.bfloat16), preferred_element_type=jnp.float32)
    return top, total, summed


def merge(unit, part, tops, totals, sums):
    top, total, summed = part
    old_top = tops[unit]
    new_top = jnp.maximum(old_top, top)
    keep = jnp.exp2((old_top - new_top) * EXP2_SCALE)
    add = jnp.exp2((top - new_top) * EXP2_SCALE)
    tops[unit] = new_top
    totals[unit] = totals[unit] * keep + total * add
    sums[unit] = sums[unit] * keep + summed * add


def for_groups(count, items, blocks_dev, body):
    def step(group, carry):
        slots = []
        for slot in range(GROUP):
            position = group * GROUP + slot
            code = items[jnp.minimum(position, count - 1)]
            unit = code // CODE
            slots.append(
                (
                    position,
                    position < count,
                    unit,
                    unit // blocks_dev,
                    unit % blocks_dev,
                    code % CODE,
                )
            )
        body(slots)
        return carry

    lax.fori_loop(0, (count + GROUP - 1) // GROUP, step, 0)


def own_kernel(
    blocks_dev,
    lists,
    lengths,
    q_in,
    k_in,
    v_in,
    tops,
    totals,
    sums,
    far_items,
    far_count,
    own_items,
    q_ref,
    k_ref,
    v_ref,
    vt_ref,
    weights_all,
    sems,
):
    copies = [
        pltpu.make_async_copy(source, target, sems.at[index])
        for index, (source, target) in enumerate(((v_in, v_ref), (q_in, q_ref), (k_in, k_ref)))
    ]
    for copy in copies:
        copy.start()
    base = lists[0, 0, 0]

    def plan_unit(unit, counts):
        head = unit // blocks_dev
        local = unit % blocks_dev

        def plan_entry(entry, counts):
            own, far = counts
            block = lists[head, local, entry] - base
            code = unit * CODE
            is_own = jnp.logical_and(block >= 0, block < blocks_dev)

            @pl.when(is_own)
            def _():
                own_items[own] = code + block

            @pl.when(jnp.logical_not(is_own))
            def _():
                far_items[far] = code + jnp.where(block < 0, block + blocks_dev, block)

            mine = is_own.astype(jnp.int32)
            return own + mine, far + 1 - mine

        return lax.fori_loop(0, lengths[head, local], plan_entry, counts)

    zero = jnp.int32(0)
    own, far = lax.fori_loop(0, HEADS * blocks_dev, plan_unit, (zero, zero))
    far_count[0] = far

    def turn(block, carry):
        for head in range(HEADS):
            lanes = slice(head * HEAD_DIM, (head + 1) * HEAD_DIM)
            vt_ref[lanes, aligned(block)] = v_ref[aligned(block), lanes].T
        return carry

    copies[0].wait()
    lax.fori_loop(0, blocks_dev, turn, 0)
    tops[...] = jnp.full(tops.shape, NEVER, jnp.float32)
    totals[...] = jnp.zeros(totals.shape, jnp.float32)
    sums[...] = jnp.zeros(sums.shape, jnp.float32)
    copies[1].wait()
    copies[2].wait()

    def top_body(slots):
        found = []
        for position, live, unit, head, local, block in slots:
            scores = score_tile(
                k_ref[aligned(block), aligned(head)], q_ref[aligned(local), aligned(head)]
            )
            found.append((unit, jnp.max(scores, axis=0, keepdims=True)))
        for unit, top in found:
            tops[unit] = jnp.maximum(tops[unit], top)

    for_groups(own, own_items, blocks_dev, top_body)

    def weights_body(slots):
        found = []
        for position, live, unit, head, local, block in slots:
            scores = score_tile(
                k_ref[aligned(block), aligned(head)], q_ref[aligned(local), aligned(head)]
            )
            top = jnp.where(live, tops[unit], -NEVER)
            weights = jnp.exp2((scores - top) * EXP2_SCALE)
            weights_all[position] = weights.astype(jnp.bfloat16)
            found.append((unit, jnp.sum(weights, axis=0, keepdims=True)))
        for unit, total in found:
            totals[unit] += total

    for_groups(own, own_items, blocks_dev, weights_body)

    def sum_body(slots):
        found = []
        for position, live, unit, head, local, block in slots:
            summed = jnp.dot(
                vt_ref[aligned(head), aligned(block)],
                weights_all[position],
                preferred_element_type=jnp.float32,
            )
            found.append((unit, summed))
        for unit, summed in found:
            sums[unit] += summed

    for_groups(own, own_items, blocks_dev, sum_body)


def middle_kernel(
    blocks_dev,
    far_items,
    far_count,
    q_ref,
    k_low,
    k_high,
    text,
    tops_in,
    totals_in,
    sums_in,
    near_out,
    weights_out,
    k_far,
    tops,
    totals,
    sums,
    near_tops,
    levels,
    item_tops,
    item_totals,
    weights_all,
    sems,
    out_sems,
):
    tokens = k_low.shape[0]
    copies = [
        pltpu.make_async_copy(k_low, k_far.at[pl.ds(0, tokens)], sems.at[0]),
        pltpu.make_async_copy(k_high, k_far.at[pl.ds(tokens, tokens)], sems.at[1]),
    ]
    for copy in copies:
        copy.start()
    tops[...] = tops_in[...]
    totals[...] = totals_in[...]
    sums[...] = sums_in[...]

    def text_head(head, carry):
        keys = text[0, :, aligned(head)]
        values_t = text[1, :, aligned(head)].T
        parts = []
        for pair in range(blocks_dev // 2):
            rows = pl.ds(pair * 2 * BLOCK, 2 * BLOCK)
            parts.append(partial_attention(keys, q_ref[rows, aligned(head)], values_t))
        for pair, (top, total, summed) in enumerate(parts):
            for side in range(2):
                unit = head * blocks_dev + pair * 2 + side
                lanes = slice(side * BLOCK, (side + 1) * BLOCK)
                merge(unit, (top[:, lanes], total[:, lanes], summed[:, lanes]), tops, totals, sums)
        return carry

    lax.fori_loop(0, HEADS, text_head, 0)
    for copy in copies:
        copy.wait()
    near_tops[...] = tops[...]
    count = far_count[0]

    def total_body(slots):
        found = []
        for position, live, unit, head, local, block in slots:
            scores = score_tile(
                k_far[aligned(block), aligned(head)], q_ref[aligned(local), aligned(head)]
            )
            top = jnp.max(scores, axis=0, keepdims=True)
            total = jnp.sum(jnp.exp2((scores - top) * EXP2_SCALE), axis=0, keepdims=True)
            found.append((unit, position, jnp.where(live, top, NEVER), total))
        for unit, position, top, total in found:
            item_tops[position] = top
            item_totals[position] = total
            tops[unit] = jnp.maximum(tops[unit], top)

    for_groups(count, far_items, blocks_dev, total_body)
    totals[...] = totals[...] * jnp.exp2((near_tops[...] - tops[...]) * EXP2_SCALE)

    def fold_body(slots):
        found = []
        for position, live, unit, head, local, block in slots:
            add = jnp.exp2((item_tops[position] - tops[unit]) * EXP2_SCALE)
            found.append((unit, item_totals[position] * add))
        for unit, total in found:
            totals[unit] += total

    for_groups(count, far_items, blocks_dev, fold_body)
    levels[...] = tops[...] * EXP2_SCALE + jnp.log2(totals[...])

    def weights_body(slots):
        for position, live, unit, head, local, block in slots:
            scores = score_tile(
                k_far[aligned(block), aligned(head)], q_ref[aligned(local), aligned(head)]
            )
            level = jnp.where(live, levels[unit], -NEVER)
            weights = jnp.exp2(scores * EXP2_SCALE - level).astype(jnp.bfloat16)
            weights_all[position] = weights.T
        first = pl.multiple_of(slots[0][0], GROUP)
        part = pl.ds(first, GROUP)
        pltpu.make_async_copy(
            weights_all.at[part], weights_out.at[part], out_sems.at[first // GROUP]
        ).start()

    for_groups(count, far_items, blocks_dev, weights_body)

    def near_rows(local, carry):
        for head in range(HEADS):
            unit = head * blocks_dev + local
            factor = jnp.exp2(near_tops[unit] * EXP2_SCALE - levels[unit])
            near_out[aligned(local), head * HEAD_DIM : (head + 1) * HEAD_DIM] = (
                sums[unit] * factor
            ).T
        return carry

    lax.fori_loop(0, blocks_dev, near_rows, 0)

    def settle(group, carry):
        part = pl.ds(pl.multiple_of(group * GROUP, GROUP), GROUP)
        pltpu.make_async_copy(weights_all.at[part], weights_out.at[part], out_sems.at[group]).wait()
        return carry

    lax.fori_loop(0, (count + GROUP - 1) // GROUP, settle, 0)


def last_kernel(
    blocks_dev,
    far_items,
    far_count,
    near,
    weights,
    v_low,
    v_high,
    out_ref,
    v_far,
    total_rows,
    weights_all,
    sems,
    weight_sems,
):
    tokens = v_low.shape[0]
    count = far_count[0]
    groups = (count + GROUP - 1) // GROUP

    def weight_copy(group):
        part = pl.ds(pl.multiple_of(group * GROUP, GROUP), GROUP)
        return pltpu.make_async_copy(weights.at[part], weights_all.at[part], weight_sems.at[group])

    copies = [
        pltpu.make_async_copy(v_low, v_far.at[pl.ds(0, tokens)], sems.at[0]),
        pltpu.make_async_copy(v_high, v_far.at[pl.ds(tokens, tokens)], sems.at[1]),
        pltpu.make_async_copy(near, total_rows, sems.at[2]),
    ]
    for copy in copies:
        copy.start()

    def begin(group, carry):
        weight_copy(group).start()
        return carry

    lax.fori_loop(0, groups, begin, 0)
    for copy in copies:
        copy.wait()

    def body(slots):
        weight_copy(slots[0][0] // GROUP).wait()
        parts = []
        for position, live, unit, head, local, block in slots:
            parts.append(
                jnp.dot(
                    weights_all[position],
                    v_far[aligned(block), aligned(head)],
                    preferred_element_type=jnp.float32,
                )
            )
        for slot, part in zip(slots, parts):
            total_rows[aligned(slot[4]), aligned(slot[3])] += part

    for_groups(count, far_items, blocks_dev, body)
    out_ref[...] = total_rows[...].astype(jnp.bfloat16)


def text_step(text, distance):
    count = lax.axis_size("seq")
    pairs = [(i, i ^ distance) for i in range(count)]
    return jnp.concatenate([text, lax.ppermute(text, "seq", pairs)], axis=1)


def on_device(queries, video_keys, video_values, text_keys, text_values, block_lists, list_lengths):
    tokens = queries.shape[0]
    columns = queries.shape[1]
    blocks_dev = tokens // BLOCK
    count = lax.axis_size("seq")
    assert blocks_dev == REACH and 2 * blocks_dev <= CODE and count & (count - 1) == 0
    units = HEADS * blocks_dev
    longest = block_lists.shape[2]
    forward = [(i, i + 1) for i in range(count - 1)]
    backward = [(target, source) for source, target in forward]

    k_low = lax.ppermute(video_keys, "seq", forward)
    k_high = lax.ppermute(video_keys, "seq", backward)
    text = text_step(jnp.stack([text_keys, text_values], 0), 2)
    v_low = lax.ppermute(video_values, "seq", forward)
    v_high = lax.ppermute(video_values, "seq", backward)
    distance = 4
    while distance < count:
        text = text_step(text, distance)
        distance *= 2
    text = text_step(text, 1)

    smem = pl.BlockSpec(memory_space=pltpu.SMEM)
    vmem = pl.BlockSpec(memory_space=pltpu.VMEM)
    anywhere = pl.BlockSpec(memory_space=pl.ANY)
    stat = (units, 1, BLOCK)
    squares = (units, HEAD_DIM, BLOCK)
    room = -(-units * (longest - 1) // GROUP) * GROUP
    weights_shape = (room, BLOCK, BLOCK)
    params = pltpu.CompilerParams(vmem_limit_bytes=VMEM_BYTES)

    tops, totals, sums, far_items, far_count = pl.pallas_call(
        functools.partial(own_kernel, blocks_dev),
        out_shape=(
            jax.ShapeDtypeStruct(stat, jnp.float32),
            jax.ShapeDtypeStruct(stat, jnp.float32),
            jax.ShapeDtypeStruct(squares, jnp.float32),
            jax.ShapeDtypeStruct((room,), jnp.int32),
            jax.ShapeDtypeStruct((1,), jnp.int32),
        ),
        in_specs=[smem, smem] + [anywhere] * 3,
        out_specs=(vmem, vmem, vmem, smem, smem),
        scratch_shapes=[
            pltpu.SMEM((units * longest,), jnp.int32),
            pltpu.VMEM((tokens, columns), jnp.bfloat16),
            pltpu.VMEM((tokens, columns), jnp.bfloat16),
            pltpu.VMEM((tokens, columns), jnp.bfloat16),
            pltpu.VMEM((columns, tokens), jnp.bfloat16),
            pltpu.VMEM((units * blocks_dev, BLOCK, BLOCK), jnp.bfloat16),
            pltpu.SemaphoreType.DMA((3,)),
        ],
        compiler_params=params,
        cost_estimate=pl.CostEstimate(
            flops=6_000_000_000, bytes_accessed=6_000_000, transcendentals=2_000_000
        ),
        name="own",
    )(block_lists, list_lengths, queries, video_keys, video_values)

    near, weights = pl.pallas_call(
        functools.partial(middle_kernel, blocks_dev),
        out_shape=(
            jax.ShapeDtypeStruct((tokens, columns), jnp.float32),
            jax.ShapeDtypeStruct(weights_shape, jnp.bfloat16),
        ),
        in_specs=[smem, smem, vmem, anywhere, anywhere] + [vmem] * 4,
        out_specs=(vmem, anywhere),
        scratch_shapes=[
            pltpu.VMEM((2 * tokens, columns), jnp.bfloat16),
            pltpu.VMEM(stat, jnp.float32),
            pltpu.VMEM(stat, jnp.float32),
            pltpu.VMEM(squares, jnp.float32),
            pltpu.VMEM(stat, jnp.float32),
            pltpu.VMEM(stat, jnp.float32),
            pltpu.VMEM((room, 1, BLOCK), jnp.float32),
            pltpu.VMEM((room, 1, BLOCK), jnp.float32),
            pltpu.VMEM(weights_shape, jnp.bfloat16),
            pltpu.SemaphoreType.DMA((2,)),
            pltpu.SemaphoreType.DMA((room // GROUP,)),
        ],
        compiler_params=params,
        cost_estimate=pl.CostEstimate(
            flops=8_000_000_000, bytes_accessed=12_000_000, transcendentals=5_000_000
        ),
        name="middle",
    )(far_items, far_count, queries, k_low, k_high, text, tops, totals, sums)

    return pl.pallas_call(
        functools.partial(last_kernel, blocks_dev),
        out_shape=jax.ShapeDtypeStruct((tokens, columns), jnp.bfloat16),
        in_specs=[smem, smem] + [anywhere] * 4,
        out_specs=vmem,
        scratch_shapes=[
            pltpu.VMEM((2 * tokens, columns), jnp.bfloat16),
            pltpu.VMEM((tokens, columns), jnp.float32),
            pltpu.VMEM(weights_shape, jnp.bfloat16),
            pltpu.SemaphoreType.DMA((3,)),
            pltpu.SemaphoreType.DMA((room // GROUP,)),
        ],
        compiler_params=params,
        cost_estimate=pl.CostEstimate(
            flops=1_000_000_000, bytes_accessed=9_000_000, transcendentals=0
        ),
        name="last",
    )(far_items, far_count, near, weights, v_low, v_high)


def solution(mesh):
    in_specs = (
        P(("groups", "seq"), None),
        P(("groups", "seq"), None),
        P(("groups", "seq"), None),
        P(("groups", "seq"), None),
        P(("groups", "seq"), None),
        P(None, ("groups", "seq"), None),
        P(None, ("groups", "seq")),
    )
    out_specs = P(("groups", "seq"), None)
    return jax.shard_map(
        on_device, mesh=mesh, in_specs=in_specs, out_specs=out_specs, check_vma=False
    )
```

```python
import functools
import math

import jax
import jax.numpy as jnp
from jax import lax
from jax.experimental import pallas as pl
from jax.experimental.pallas import tpu as pltpu
from jax.sharding import PartitionSpec as P

HEAD_DIM = 128
HEADS = 4
BLOCK = 128
REACH = 8
GROUP = 16
EXP2_SCALE = HEAD_DIM ** (-0.5) * math.log2(math.e)
NEVER = -1e30
NT = (((1,), (1,)), ((), ()))
VMEM_BYTES = 63 * 1024 * 1024
CODE = 64


def aligned(index):
    return pl.ds(pl.multiple_of(index * BLOCK, BLOCK), BLOCK)


def score_tile(keys, query_rows):
    return lax.dot_general(keys, query_rows, NT, preferred_element_type=jnp.float32)


def for_groups(count, items, blocks_dev, body):
    def step(group, carry):
        slots = []
        for slot in range(GROUP):
            position = group * GROUP + slot
            code = items[jnp.minimum(position, count - 1)]
            unit = code // CODE
            slots.append(
                (
                    position,
                    position < count,
                    unit,
                    unit // blocks_dev,
                    unit % blocks_dev,
                    code % CODE,
                )
            )
        body(slots)
        return carry

    lax.fori_loop(0, (count + GROUP - 1) // GROUP, step, 0)


def text_kernel(
    blocks_dev,
    lists,
    lengths,
    q_in,
    text_in,
    own_items,
    far_items,
    counts,
    tops,
    totals,
    sums,
    q_ref,
    text,
    weights_all,
    sems,
):
    copies = [
        pltpu.make_async_copy(text_in, text, sems.at[0]),
        pltpu.make_async_copy(q_in, q_ref, sems.at[1]),
    ]
    for copy in copies:
        copy.start()
    base = lists[0, 0, 0]

    def plan_unit(unit, carry):
        head = unit // blocks_dev
        local = unit % blocks_dev

        def plan_entry(entry, carry):
            own, far = carry
            block = lists[head, local, entry] - base
            code = unit * CODE
            is_own = jnp.logical_and(block >= 0, block < blocks_dev)

            @pl.when(is_own)
            def _():
                own_items[own] = code + block

            @pl.when(jnp.logical_not(is_own))
            def _():
                far_items[far] = code + jnp.where(block < 0, block + blocks_dev, block)

            mine = is_own.astype(jnp.int32)
            return own + mine, far + 1 - mine

        return lax.fori_loop(0, lengths[head, local], plan_entry, carry)

    zero = jnp.int32(0)
    own, far = lax.fori_loop(0, HEADS * blocks_dev, plan_unit, (zero, zero))
    counts[0] = own
    counts[1] = far
    for copy in copies:
        copy.wait()
    pairs = blocks_dev // 2

    def weights_head(head, carry):
        keys = text[0, :, aligned(head)]
        for pair in range(pairs):
            rows = pl.ds(pair * 2 * BLOCK, 2 * BLOCK)
            scores = score_tile(keys, q_ref[rows, aligned(head)])
            top = jnp.max(scores, axis=0, keepdims=True)
            weights = jnp.exp2((scores - top) * EXP2_SCALE)
            weights_all[head * pairs + pair] = weights.astype(jnp.bfloat16)
            total = jnp.sum(weights, axis=0, keepdims=True)
            for side in range(2):
                unit = head * blocks_dev + pair * 2 + side
                lanes = slice(side * BLOCK, (side + 1) * BLOCK)
                tops[unit] = top[:, lanes]
                totals[unit] = total[:, lanes]
        return carry

    lax.fori_loop(0, HEADS, weights_head, 0)

    def sums_head(head, carry):
        values_t = text[1, :, aligned(head)].T
        for pair in range(pairs):
            summed = jnp.dot(
                values_t, weights_all[head * pairs + pair], preferred_element_type=jnp.float32
            )
            for side in range(2):
                unit = head * blocks_dev + pair * 2 + side
                sums[unit] = summed[:, side * BLOCK : (side + 1) * BLOCK]
        return carry

    lax.fori_loop(0, HEADS, sums_head, 0)


def own_kernel(
    blocks_dev,
    own_items,
    counts,
    q_in,
    k_in,
    v_in,
    sums_in,
    text_tops,
    text_totals,
    tops,
    totals,
    sums,
    q_ref,
    k_ref,
    v_ref,
    vt_ref,
    scores_all,
    weights_all,
    sems,
):
    copies = [
        pltpu.make_async_copy(source, target, sems.at[index])
        for index, (source, target) in enumerate(((q_in, q_ref), (k_in, k_ref), (v_in, v_ref), (sums_in, sums)))
    ]
    for copy in copies:
        copy.start()
    own = counts[0]

    def turn(block, carry):
        for head in range(HEADS):
            lanes = slice(head * HEAD_DIM, (head + 1) * HEAD_DIM)
            vt_ref[lanes, aligned(block)] = v_ref[aligned(block), lanes].T
        return carry

    tops[...] = text_tops[...]
    copies[0].wait()
    copies[1].wait()

    def top_body(slots):
        found = []
        for position, live, unit, head, local, block in slots:
            scores = score_tile(
                k_ref[aligned(block), aligned(head)], q_ref[aligned(local), aligned(head)]
            )
            scores_all[position] = scores
            found.append((unit, jnp.max(scores, axis=0, keepdims=True)))
        for unit, top in found:
            tops[unit] = jnp.maximum(tops[unit], top)

    for_groups(own, own_items, blocks_dev, top_body)
    factor = jnp.exp2((text_tops[...] - tops[...]) * EXP2_SCALE)
    totals[...] = text_totals[...] * factor
    copies[3].wait()
    sums[...] = sums[...] * factor

    def weights_body(slots):
        found = []
        for position, live, unit, head, local, block in slots:
            top = jnp.where(live, tops[unit], -NEVER)
            weights = jnp.exp2((scores_all[position] - top) * EXP2_SCALE)
            weights_all[position] = weights.astype(jnp.bfloat16)
            found.append((unit, jnp.sum(weights, axis=0, keepdims=True)))
        for unit, total in found:
            totals[unit] += total

    for_groups(own, own_items, blocks_dev, weights_body)

    def sum_body(slots):
        found = []
        for position, live, unit, head, local, block in slots:
            summed = jnp.dot(
                vt_ref[aligned(head), aligned(block)],
                weights_all[position],
                preferred_element_type=jnp.float32,
            )
            found.append((unit, summed))
        for unit, summed in found:
            sums[unit] += summed

    copies[2].wait()
    lax.fori_loop(0, blocks_dev, turn, 0)
    for_groups(own, own_items, blocks_dev, sum_body)


def middle_kernel(
    blocks_dev,
    far_items,
    counts,
    q_ref,
    k_low,
    k_high,
    near_tops,
    near_totals,
    sums,
    near_out,
    weights_out,
    k_far,
    tops,
    totals,
    levels,
    item_tops,
    item_totals,
    scores_all,
    weights_all,
    sems,
    out_sems,
):
    tokens = k_low.shape[0]
    copies = [
        pltpu.make_async_copy(k_low, k_far.at[pl.ds(0, tokens)], sems.at[0]),
        pltpu.make_async_copy(k_high, k_far.at[pl.ds(tokens, tokens)], sems.at[1]),
    ]
    for copy in copies:
        copy.start()
    tops[...] = near_tops[...]
    totals[...] = near_totals[...]
    for copy in copies:
        copy.wait()
    count = counts[1]

    def total_body(slots):
        found = []
        for position, live, unit, head, local, block in slots:
            scores = score_tile(
                k_far[aligned(block), aligned(head)], q_ref[aligned(local), aligned(head)]
            )
            top = jnp.max(scores, axis=0, keepdims=True)
            total = jnp.sum(jnp.exp2((scores - top) * EXP2_SCALE), axis=0, keepdims=True)
            scores_all[position] = scores
            found.append((unit, position, jnp.where(live, top, NEVER), total))
        for unit, position, top, total in found:
            item_tops[position] = top
            item_totals[position] = total
            tops[unit] = jnp.maximum(tops[unit], top)

    for_groups(count, far_items, blocks_dev, total_body)
    totals[...] = totals[...] * jnp.exp2((near_tops[...] - tops[...]) * EXP2_SCALE)

    def fold_body(slots):
        found = []
        for position, live, unit, head, local, block in slots:
            add = jnp.exp2((item_tops[position] - tops[unit]) * EXP2_SCALE)
            found.append((unit, item_totals[position] * add))
        for unit, total in found:
            totals[unit] += total

    for_groups(count, far_items, blocks_dev, fold_body)
    levels[...] = tops[...] * EXP2_SCALE + jnp.log2(totals[...])

    def weights_body(slots):
        for position, live, unit, head, local, block in slots:
            level = jnp.where(live, levels[unit], -NEVER)
            weights = jnp.exp2(scores_all[position] * EXP2_SCALE - level).astype(jnp.bfloat16)
            weights_all[position] = weights.T
        first = pl.multiple_of(slots[0][0], GROUP)
        part = pl.ds(first, GROUP)
        pltpu.make_async_copy(
            weights_all.at[part], weights_out.at[part], out_sems.at[first // GROUP]
        ).start()

    for_groups(count, far_items, blocks_dev, weights_body)

    def near_rows(local, carry):
        for head in range(HEADS):
            unit = head * blocks_dev + local
            factor = jnp.exp2(near_tops[unit] * EXP2_SCALE - levels[unit])
            near_out[aligned(local), head * HEAD_DIM : (head + 1) * HEAD_DIM] = (
                sums[unit] * factor
            ).T
        return carry

    lax.fori_loop(0, blocks_dev, near_rows, 0)

    def settle(group, carry):
        part = pl.ds(pl.multiple_of(group * GROUP, GROUP), GROUP)
        pltpu.make_async_copy(weights_all.at[part], weights_out.at[part], out_sems.at[group]).wait()
        return carry

    lax.fori_loop(0, (count + GROUP - 1) // GROUP, settle, 0)


def last_kernel(
    blocks_dev,
    far_items,
    counts,
    near,
    weights,
    v_low,
    v_high,
    out_ref,
    v_far,
    total_rows,
    weights_all,
    sems,
    weight_sems,
):
    tokens = v_low.shape[0]
    count = counts[1]
    groups = (count + GROUP - 1) // GROUP

    def weight_copy(group):
        part = pl.ds(pl.multiple_of(group * GROUP, GROUP), GROUP)
        return pltpu.make_async_copy(weights.at[part], weights_all.at[part], weight_sems.at[group])

    copies = [
        pltpu.make_async_copy(v_low, v_far.at[pl.ds(0, tokens)], sems.at[0]),
        pltpu.make_async_copy(v_high, v_far.at[pl.ds(tokens, tokens)], sems.at[1]),
        pltpu.make_async_copy(near, total_rows, sems.at[2]),
    ]
    for copy in copies:
        copy.start()

    def begin(group, carry):
        weight_copy(group).start()
        return carry

    lax.fori_loop(0, groups, begin, 0)
    for copy in copies:
        copy.wait()

    def body(slots):
        weight_copy(slots[0][0] // GROUP).wait()
        parts = []
        for position, live, unit, head, local, block in slots:
            parts.append(
                jnp.dot(
                    weights_all[position],
                    v_far[aligned(block), aligned(head)],
                    preferred_element_type=jnp.float32,
                )
            )
        for slot, part in zip(slots, parts):
            total_rows[aligned(slot[4]), aligned(slot[3])] += part

    for_groups(count, far_items, blocks_dev, body)
    out_ref[...] = total_rows[...].astype(jnp.bfloat16)


def text_step(text, distances):
    count = lax.axis_size("seq")
    parts = [text]
    for distance in distances:
        parts.append(lax.ppermute(text, "seq", [(i, i ^ distance) for i in range(count)]))
    return jnp.concatenate(parts, axis=1)


def on_device(queries, video_keys, video_values, text_keys, text_values, block_lists, list_lengths):
    tokens = queries.shape[0]
    columns = queries.shape[1]
    blocks_dev = tokens // BLOCK
    count = lax.axis_size("seq")
    assert blocks_dev == REACH and 2 * blocks_dev <= CODE and count & (count - 1) == 0
    units = HEADS * blocks_dev
    longest = block_lists.shape[2]
    forward = [(i, i + 1) for i in range(count - 1)]
    backward = [(target, source) for source, target in forward]

    smem = pl.BlockSpec(memory_space=pltpu.SMEM)
    vmem = pl.BlockSpec(memory_space=pltpu.VMEM)
    anywhere = pl.BlockSpec(memory_space=pl.ANY)
    stat = (units, 1, BLOCK)
    squares = (units, HEAD_DIM, BLOCK)
    room = -(-units * (longest - 1) // GROUP) * GROUP
    weights_shape = (room, BLOCK, BLOCK)
    params = pltpu.CompilerParams(vmem_limit_bytes=VMEM_BYTES)

    text = text_step(jnp.stack([text_keys, text_values], 0), (2,))
    keys, text = lax.optimization_barrier((video_keys, text))
    k_low = lax.ppermute(keys, "seq", forward)
    k_high = lax.ppermute(keys, "seq", backward)
    text = text_step(text, (4, 8, 12) if count >= 16 else (4,) if count == 8 else ())
    distance = 16
    while distance < count:
        text = text_step(text, (distance,))
        distance *= 2
    text = text_step(text, (1,))

    own_items, far_items, counts, text_tops, text_totals, text_sums = pl.pallas_call(
        functools.partial(text_kernel, blocks_dev),
        out_shape=(
            jax.ShapeDtypeStruct((units * blocks_dev,), jnp.int32),
            jax.ShapeDtypeStruct((room,), jnp.int32),
            jax.ShapeDtypeStruct((2,), jnp.int32),
            jax.ShapeDtypeStruct(stat, jnp.float32),
            jax.ShapeDtypeStruct(stat, jnp.float32),
            jax.ShapeDtypeStruct(squares, jnp.float32),
        ),
        in_specs=[smem, smem, anywhere, anywhere],
        out_specs=(smem, smem, smem, vmem, vmem, vmem),
        scratch_shapes=[
            pltpu.VMEM((tokens, columns), jnp.bfloat16),
            pltpu.VMEM(text.shape, jnp.bfloat16),
            pltpu.VMEM((units // 2, text.shape[1], 2 * BLOCK), jnp.bfloat16),
            pltpu.SemaphoreType.DMA((2,)),
        ],
        compiler_params=params,
        cost_estimate=pl.CostEstimate(flops=1_000_000, bytes_accessed=10_000, transcendentals=0),
        name="text",
    )(block_lists, list_lengths, queries, text)

    values, own_items = lax.optimization_barrier((video_values, own_items))
    v_low = lax.ppermute(values, "seq", forward)
    v_high = lax.ppermute(values, "seq", backward)

    tops, totals, sums = pl.pallas_call(
        functools.partial(own_kernel, blocks_dev),
        out_shape=(
            jax.ShapeDtypeStruct(stat, jnp.float32),
            jax.ShapeDtypeStruct(stat, jnp.float32),
            jax.ShapeDtypeStruct(squares, jnp.float32),
        ),
        in_specs=[smem, smem] + [anywhere] * 4 + [vmem] * 2,
        out_specs=(vmem, vmem, vmem),
        scratch_shapes=[
            pltpu.VMEM((tokens, columns), jnp.bfloat16),
            pltpu.VMEM((tokens, columns), jnp.bfloat16),
            pltpu.VMEM((tokens, columns), jnp.bfloat16),
            pltpu.VMEM((columns, tokens), jnp.bfloat16),
            pltpu.VMEM((units * blocks_dev, BLOCK, BLOCK), jnp.float32),
            pltpu.VMEM((units * blocks_dev, BLOCK, BLOCK), jnp.bfloat16),
            pltpu.SemaphoreType.DMA((4,)),
        ],
        compiler_params=params,
        cost_estimate=pl.CostEstimate(flops=1_000_000, bytes_accessed=10_000, transcendentals=0),
        name="own",
    )(
        own_items,
        counts,
        queries,
        video_keys,
        video_values,
        text_sums,
        text_tops,
        text_totals,
    )

    near, weights = pl.pallas_call(
        functools.partial(middle_kernel, blocks_dev),
        out_shape=(
            jax.ShapeDtypeStruct((tokens, columns), jnp.float32),
            jax.ShapeDtypeStruct(weights_shape, jnp.bfloat16),
        ),
        in_specs=[smem, smem, vmem, anywhere, anywhere] + [vmem] * 3,
        out_specs=(vmem, anywhere),
        scratch_shapes=[
            pltpu.VMEM((2 * tokens, columns), jnp.bfloat16),
            pltpu.VMEM(stat, jnp.float32),
            pltpu.VMEM(stat, jnp.float32),
            pltpu.VMEM(stat, jnp.float32),
            pltpu.VMEM((room, 1, BLOCK), jnp.float32),
            pltpu.VMEM((room, 1, BLOCK), jnp.float32),
            pltpu.VMEM(weights_shape, jnp.float32),
            pltpu.VMEM(weights_shape, jnp.bfloat16),
            pltpu.SemaphoreType.DMA((2,)),
            pltpu.SemaphoreType.DMA((room // GROUP,)),
        ],
        compiler_params=params,
        cost_estimate=pl.CostEstimate(
            flops=1_000_000, bytes_accessed=10_000, transcendentals=0
        ),
        name="middle",
    )(far_items, counts, queries, k_low, k_high, tops, totals, sums)

    return pl.pallas_call(
        functools.partial(last_kernel, blocks_dev),
        out_shape=jax.ShapeDtypeStruct((tokens, columns), jnp.bfloat16),
        in_specs=[smem, smem] + [anywhere] * 4,
        out_specs=vmem,
        scratch_shapes=[
            pltpu.VMEM((2 * tokens, columns), jnp.bfloat16),
            pltpu.VMEM((tokens, columns), jnp.float32),
            pltpu.VMEM(weights_shape, jnp.bfloat16),
            pltpu.SemaphoreType.DMA((3,)),
            pltpu.SemaphoreType.DMA((room // GROUP,)),
        ],
        compiler_params=params,
        cost_estimate=pl.CostEstimate(
            flops=1_000_000_000, bytes_accessed=9_000_000, transcendentals=0
        ),
        name="last",
    )(far_items, counts, near, weights, v_low, v_high)


def solution(mesh):
    in_specs = (
        P(("groups", "seq"), None),
        P(("groups", "seq"), None),
        P(("groups", "seq"), None),
        P(("groups", "seq"), None),
        P(("groups", "seq"), None),
        P(None, ("groups", "seq"), None),
        P(None, ("groups", "seq")),
    )
    out_specs = P(("groups", "seq"), None)
    return jax.shard_map(
        on_device, mesh=mesh, in_specs=in_specs, out_specs=out_specs, check_vma=False
    )
```

```python
import functools
import math

import jax
import jax.numpy as jnp
from jax import lax
from jax.experimental import pallas as pl
from jax.experimental.pallas import tpu as pltpu
from jax.sharding import PartitionSpec as P

HEAD_DIM = 128
HEADS = 4
BLOCK = 128
REACH = 8
GROUP = 16
EXP2_SCALE = HEAD_DIM ** (-0.5) * math.log2(math.e)
NEVER = -1e30
NT = (((1,), (1,)), ((), ()))
VMEM_BYTES = 63 * 1024 * 1024
CODE = 64


def aligned(index):
    return pl.ds(pl.multiple_of(index * BLOCK, BLOCK), BLOCK)


def score_tile(keys, query_rows):
    return lax.dot_general(keys, query_rows, NT, preferred_element_type=jnp.float32)


def for_groups(count, items, blocks_dev, body):
    def step(group, carry):
        slots = []
        for slot in range(GROUP):
            position = group * GROUP + slot
            code = items[jnp.minimum(position, count - 1)]
            unit = code // CODE
            slots.append(
                (
                    position,
                    position < count,
                    unit,
                    unit // blocks_dev,
                    unit % blocks_dev,
                    code % CODE,
                )
            )
        body(slots)
        return carry

    lax.fori_loop(0, (count + GROUP - 1) // GROUP, step, 0)


def text_kernel(
    blocks_dev,
    lists,
    lengths,
    q_in,
    text_in,
    near_items,
    far_items,
    counts,
    tops,
    totals,
    sums,
    q_ref,
    text,
    weights_all,
    sems,
):
    copies = [
        pltpu.make_async_copy(text_in, text, sems.at[0]),
        pltpu.make_async_copy(q_in, q_ref, sems.at[1]),
    ]
    for copy in copies:
        copy.start()
    base = lists[0, 0, 0]
    odd = (base // blocks_dev) % 2 == 1

    def plan_unit(unit, carry):
        head = unit // blocks_dev
        local = unit % blocks_dev

        def plan_entry(entry, carry):
            near, far = carry
            block = lists[head, local, entry] - base
            is_low = block < 0
            is_high = block >= blocks_dev
            is_outer = jnp.where(odd, is_high, is_low)
            is_inner = jnp.where(odd, is_low, is_high)
            shift = jnp.where(is_low, blocks_dev, jnp.where(is_high, -blocks_dev, 0))
            code = unit * CODE + block + shift

            @pl.when(is_outer)
            def _():
                far_items[far] = code

            @pl.when(jnp.logical_not(is_outer))
            def _():
                near_items[near] = code + jnp.where(is_inner, blocks_dev, 0)

            outer = is_outer.astype(jnp.int32)
            return near + 1 - outer, far + outer

        return lax.fori_loop(0, lengths[head, local], plan_entry, carry)

    zero = jnp.int32(0)
    near, far = lax.fori_loop(0, HEADS * blocks_dev, plan_unit, (zero, zero))
    counts[0] = near
    counts[1] = far
    for copy in copies:
        copy.wait()
    pairs = blocks_dev // 2

    def weights_head(head, carry):
        keys = text[0, :, aligned(head)]
        for pair in range(pairs):
            rows = pl.ds(pair * 2 * BLOCK, 2 * BLOCK)
            scores = score_tile(keys, q_ref[rows, aligned(head)])
            top = jnp.max(scores, axis=0, keepdims=True)
            weights = jnp.exp2((scores - top) * EXP2_SCALE)
            weights_all[head * pairs + pair] = weights.astype(jnp.bfloat16)
            total = jnp.sum(weights, axis=0, keepdims=True)
            for side in range(2):
                unit = head * blocks_dev + pair * 2 + side
                lanes = slice(side * BLOCK, (side + 1) * BLOCK)
                tops[unit] = top[:, lanes]
                totals[unit] = total[:, lanes]
        return carry

    lax.fori_loop(0, HEADS, weights_head, 0)

    def sums_head(head, carry):
        values_t = text[1, :, aligned(head)].T
        for pair in range(pairs):
            summed = jnp.dot(
                values_t, weights_all[head * pairs + pair], preferred_element_type=jnp.float32
            )
            for side in range(2):
                unit = head * blocks_dev + pair * 2 + side
                sums[unit] = summed[:, side * BLOCK : (side + 1) * BLOCK]
        return carry

    lax.fori_loop(0, HEADS, sums_head, 0)


def near_kernel(
    blocks_dev,
    near_items,
    counts,
    q_in,
    k_in,
    v_in,
    k_inner,
    v_inner,
    sums_in,
    text_tops,
    text_totals,
    tops,
    totals,
    sums,
    q_ref,
    k_ref,
    v_ref,
    vt_ref,
    scores_all,
    weights_all,
    sems,
):
    tokens = k_in.shape[0]
    first, second = pl.ds(0, tokens), pl.ds(tokens, tokens)
    moves = (
        (q_in, q_ref),
        (k_in, k_ref.at[first]),
        (k_inner, k_ref.at[second]),
        (v_in, v_ref.at[first]),
        (v_inner, v_ref.at[second]),
        (sums_in, sums),
    )
    copies = [
        pltpu.make_async_copy(source, target, sems.at[index])
        for index, (source, target) in enumerate(moves)
    ]
    for copy in copies:
        copy.start()
    count = counts[0]

    def turn(block, carry):
        for head in range(HEADS):
            lanes = slice(head * HEAD_DIM, (head + 1) * HEAD_DIM)
            vt_ref[lanes, aligned(block)] = v_ref[aligned(block), lanes].T
        return carry

    tops[...] = text_tops[...]
    for copy in copies[:3]:
        copy.wait()

    def top_body(slots):
        found = []
        for position, live, unit, head, local, block in slots:
            scores = score_tile(
                k_ref[aligned(block), aligned(head)], q_ref[aligned(local), aligned(head)]
            )
            scores_all[position] = scores
            found.append((unit, jnp.max(scores, axis=0, keepdims=True)))
        for unit, top in found:
            tops[unit] = jnp.maximum(tops[unit], top)

    for_groups(count, near_items, blocks_dev, top_body)
    factor = jnp.exp2((text_tops[...] - tops[...]) * EXP2_SCALE)
    totals[...] = text_totals[...] * factor
    copies[5].wait()
    sums[...] = sums[...] * factor

    def weights_body(slots):
        found = []
        for position, live, unit, head, local, block in slots:
            top = jnp.where(live, tops[unit], -NEVER)
            weights = jnp.exp2((scores_all[position] - top) * EXP2_SCALE)
            weights_all[position] = weights.astype(jnp.bfloat16)
            found.append((unit, jnp.sum(weights, axis=0, keepdims=True)))
        for unit, total in found:
            totals[unit] += total

    for_groups(count, near_items, blocks_dev, weights_body)

    def sum_body(slots):
        found = []
        for position, live, unit, head, local, block in slots:
            summed = jnp.dot(
                vt_ref[aligned(head), aligned(block)],
                weights_all[position],
                preferred_element_type=jnp.float32,
            )
            found.append((unit, summed))
        for unit, summed in found:
            sums[unit] += summed

    copies[3].wait()
    copies[4].wait()
    lax.fori_loop(0, 2 * blocks_dev, turn, 0)
    for_groups(count, near_items, blocks_dev, sum_body)


def middle_kernel(
    blocks_dev,
    far_items,
    counts,
    q_ref,
    k_far,
    near_tops,
    near_totals,
    sums,
    near_out,
    weights_out,
    tops,
    totals,
    levels,
    item_tops,
    item_totals,
    scores_all,
    weights_all,
    out_sems,
):
    tops[...] = near_tops[...]
    totals[...] = near_totals[...]
    count = counts[1]

    def total_body(slots):
        found = []
        for position, live, unit, head, local, block in slots:
            scores = score_tile(
                k_far[aligned(block), aligned(head)], q_ref[aligned(local), aligned(head)]
            )
            top = jnp.max(scores, axis=0, keepdims=True)
            total = jnp.sum(jnp.exp2((scores - top) * EXP2_SCALE), axis=0, keepdims=True)
            scores_all[position] = scores
            found.append((unit, position, jnp.where(live, top, NEVER), total))
        for unit, position, top, total in found:
            item_tops[position] = top
            item_totals[position] = total
            tops[unit] = jnp.maximum(tops[unit], top)

    for_groups(count, far_items, blocks_dev, total_body)
    totals[...] = totals[...] * jnp.exp2((near_tops[...] - tops[...]) * EXP2_SCALE)

    def fold_body(slots):
        found = []
        for position, live, unit, head, local, block in slots:
            add = jnp.exp2((item_tops[position] - tops[unit]) * EXP2_SCALE)
            found.append((unit, item_totals[position] * add))
        for unit, total in found:
            totals[unit] += total

    for_groups(count, far_items, blocks_dev, fold_body)
    levels[...] = tops[...] * EXP2_SCALE + jnp.log2(totals[...])

    def weights_body(slots):
        for position, live, unit, head, local, block in slots:
            level = jnp.where(live, levels[unit], -NEVER)
            weights = jnp.exp2(scores_all[position] * EXP2_SCALE - level).astype(jnp.bfloat16)
            weights_all[position] = weights.T
        first = pl.multiple_of(slots[0][0], GROUP)
        part = pl.ds(first, GROUP)
        pltpu.make_async_copy(
            weights_all.at[part], weights_out.at[part], out_sems.at[first // GROUP]
        ).start()

    for_groups(count, far_items, blocks_dev, weights_body)

    def near_rows(local, carry):
        for head in range(HEADS):
            unit = head * blocks_dev + local
            factor = jnp.exp2(near_tops[unit] * EXP2_SCALE - levels[unit])
            near_out[aligned(local), head * HEAD_DIM : (head + 1) * HEAD_DIM] = (
                sums[unit] * factor
            ).T
        return carry

    lax.fori_loop(0, blocks_dev, near_rows, 0)

    def settle(group, carry):
        part = pl.ds(pl.multiple_of(group * GROUP, GROUP), GROUP)
        pltpu.make_async_copy(weights_all.at[part], weights_out.at[part], out_sems.at[group]).wait()
        return carry

    lax.fori_loop(0, (count + GROUP - 1) // GROUP, settle, 0)


def last_kernel(
    blocks_dev,
    far_items,
    counts,
    near,
    weights,
    v_outer,
    out_ref,
    v_far,
    total_rows,
    weights_all,
    sems,
    weight_sems,
):
    count = counts[1]
    groups = (count + GROUP - 1) // GROUP

    def weight_copy(group):
        part = pl.ds(pl.multiple_of(group * GROUP, GROUP), GROUP)
        return pltpu.make_async_copy(weights.at[part], weights_all.at[part], weight_sems.at[group])

    copies = [
        pltpu.make_async_copy(v_outer, v_far, sems.at[0]),
        pltpu.make_async_copy(near, total_rows, sems.at[1]),
    ]
    for copy in copies:
        copy.start()

    def begin(group, carry):
        weight_copy(group).start()
        return carry

    lax.fori_loop(0, groups, begin, 0)
    for copy in copies:
        copy.wait()

    def body(slots):
        weight_copy(slots[0][0] // GROUP).wait()
        parts = []
        for position, live, unit, head, local, block in slots:
            parts.append(
                jnp.dot(
                    weights_all[position],
                    v_far[aligned(block), aligned(head)],
                    preferred_element_type=jnp.float32,
                )
            )
        for slot, part in zip(slots, parts):
            total_rows[aligned(slot[4]), aligned(slot[3])] += part

    for_groups(count, far_items, blocks_dev, body)
    out_ref[...] = total_rows[...].astype(jnp.bfloat16)


def text_step(text, distances):
    count = lax.axis_size("seq")
    parts = [text]
    for distance in distances:
        parts.append(lax.ppermute(text, "seq", [(i, i ^ distance) for i in range(count)]))
    return jnp.concatenate(parts, axis=1)


def on_device(queries, video_keys, video_values, text_keys, text_values, block_lists, list_lengths):
    tokens = queries.shape[0]
    columns = queries.shape[1]
    blocks_dev = tokens // BLOCK
    count = lax.axis_size("seq")
    assert blocks_dev == REACH and 2 * blocks_dev <= CODE and count & (count - 1) == 0
    units = HEADS * blocks_dev
    longest = block_lists.shape[2]
    inner = [(i, i ^ 1) for i in range(count)]
    outer = [(i, i + 1) for i in range(1, count - 1, 2)]
    outer += [(target, source) for source, target in outer]

    smem = pl.BlockSpec(memory_space=pltpu.SMEM)
    vmem = pl.BlockSpec(memory_space=pltpu.VMEM)
    anywhere = pl.BlockSpec(memory_space=pl.ANY)
    stat = (units, 1, BLOCK)
    squares = (units, HEAD_DIM, BLOCK)
    room = -(-units * (longest - 1) // GROUP) * GROUP
    near_room = -(-units * longest // GROUP) * GROUP
    weights_shape = (room, BLOCK, BLOCK)
    near_shape = (near_room, BLOCK, BLOCK)
    params = pltpu.CompilerParams(vmem_limit_bytes=VMEM_BYTES)

    text = text_step(jnp.stack([text_keys, text_values], 0), (2,))
    keys, text = lax.optimization_barrier((video_keys, text))
    k_outer = lax.ppermute(keys, "seq", outer)
    k_inner = lax.ppermute(video_keys, "seq", inner)
    v_inner = lax.ppermute(video_values, "seq", inner)
    text = text_step(text, (4, 8, 12) if count >= 16 else (4,) if count == 8 else ())
    distance = 16
    while distance < count:
        text = text_step(text, (distance,))
        distance *= 2
    text = text_step(text, (1,))

    near_items, far_items, counts, text_tops, text_totals, text_sums = pl.pallas_call(
        functools.partial(text_kernel, blocks_dev),
        out_shape=(
            jax.ShapeDtypeStruct((near_room,), jnp.int32),
            jax.ShapeDtypeStruct((room,), jnp.int32),
            jax.ShapeDtypeStruct((2,), jnp.int32),
            jax.ShapeDtypeStruct(stat, jnp.float32),
            jax.ShapeDtypeStruct(stat, jnp.float32),
            jax.ShapeDtypeStruct(squares, jnp.float32),
        ),
        in_specs=[smem, smem, anywhere, anywhere],
        out_specs=(smem, smem, smem, vmem, vmem, vmem),
        scratch_shapes=[
            pltpu.VMEM((tokens, columns), jnp.bfloat16),
            pltpu.VMEM(text.shape, jnp.bfloat16),
            pltpu.VMEM((units // 2, text.shape[1], 2 * BLOCK), jnp.bfloat16),
            pltpu.SemaphoreType.DMA((2,)),
        ],
        compiler_params=params,
        cost_estimate=pl.CostEstimate(flops=1_000_000, bytes_accessed=10_000, transcendentals=0),
        name="text",
    )(block_lists, list_lengths, queries, text)

    values, near_items = lax.optimization_barrier((video_values, near_items))
    v_outer = lax.ppermute(values, "seq", outer)

    tops, totals, sums = pl.pallas_call(
        functools.partial(near_kernel, blocks_dev),
        out_shape=(
            jax.ShapeDtypeStruct(stat, jnp.float32),
            jax.ShapeDtypeStruct(stat, jnp.float32),
            jax.ShapeDtypeStruct(squares, jnp.float32),
        ),
        in_specs=[smem, smem] + [anywhere] * 6 + [vmem] * 2,
        out_specs=(vmem, vmem, vmem),
        scratch_shapes=[
            pltpu.VMEM((tokens, columns), jnp.bfloat16),
            pltpu.VMEM((2 * tokens, columns), jnp.bfloat16),
            pltpu.VMEM((2 * tokens, columns), jnp.bfloat16),
            pltpu.VMEM((columns, 2 * tokens), jnp.bfloat16),
            pltpu.VMEM(near_shape, jnp.float32),
            pltpu.VMEM(near_shape, jnp.bfloat16),
            pltpu.SemaphoreType.DMA((6,)),
        ],
        compiler_params=params,
        cost_estimate=pl.CostEstimate(flops=1_000_000, bytes_accessed=10_000, transcendentals=0),
        name="own",
    )(
        near_items,
        counts,
        queries,
        video_keys,
        video_values,
        k_inner,
        v_inner,
        text_sums,
        text_tops,
        text_totals,
    )

    near, weights = pl.pallas_call(
        functools.partial(middle_kernel, blocks_dev),
        out_shape=(
            jax.ShapeDtypeStruct((tokens, columns), jnp.float32),
            jax.ShapeDtypeStruct(weights_shape, jnp.bfloat16),
        ),
        in_specs=[smem, smem] + [vmem] * 5,
        out_specs=(vmem, anywhere),
        scratch_shapes=[
            pltpu.VMEM(stat, jnp.float32),
            pltpu.VMEM(stat, jnp.float32),
            pltpu.VMEM(stat, jnp.float32),
            pltpu.VMEM((room, 1, BLOCK), jnp.float32),
            pltpu.VMEM((room, 1, BLOCK), jnp.float32),
            pltpu.VMEM(weights_shape, jnp.float32),
            pltpu.VMEM(weights_shape, jnp.bfloat16),
            pltpu.SemaphoreType.DMA((room // GROUP,)),
        ],
        compiler_params=params,
        cost_estimate=pl.CostEstimate(
            flops=1_000_000, bytes_accessed=10_000, transcendentals=0
        ),
        name="middle",
    )(far_items, counts, queries, k_outer, tops, totals, sums)

    return pl.pallas_call(
        functools.partial(last_kernel, blocks_dev),
        out_shape=jax.ShapeDtypeStruct((tokens, columns), jnp.bfloat16),
        in_specs=[smem, smem] + [anywhere] * 3,
        out_specs=vmem,
        scratch_shapes=[
            pltpu.VMEM((tokens, columns), jnp.bfloat16),
            pltpu.VMEM((tokens, columns), jnp.float32),
            pltpu.VMEM(weights_shape, jnp.bfloat16),
            pltpu.SemaphoreType.DMA((2,)),
            pltpu.SemaphoreType.DMA((room // GROUP,)),
        ],
        compiler_params=params,
        cost_estimate=pl.CostEstimate(
            flops=1_000_000_000, bytes_accessed=9_000_000, transcendentals=0
        ),
        name="last",
    )(far_items, counts, near, weights, v_outer)


def solution(mesh):
    in_specs = (
        P(("groups", "seq"), None),
        P(("groups", "seq"), None),
        P(("groups", "seq"), None),
        P(("groups", "seq"), None),
        P(("groups", "seq"), None),
        P(None, ("groups", "seq"), None),
        P(None, ("groups", "seq")),
    )
    out_specs = P(("groups", "seq"), None)
    return jax.shard_map(
        on_device, mesh=mesh, in_specs=in_specs, out_specs=out_specs, check_vma=False
    )
```

```python
import functools
import math

import jax
import jax.numpy as jnp
from jax import lax
from jax.experimental import pallas as pl
from jax.experimental.pallas import tpu as pltpu
from jax.sharding import PartitionSpec as P

HEAD_DIM = 128
HEADS = 4
BLOCK = 128
REACH = 8
GROUP = 24
EXP2_SCALE = HEAD_DIM ** (-0.5) * math.log2(math.e)
NEVER = -1e30
NT = (((1,), (1,)), ((), ()))
VMEM_BYTES = 63 * 1024 * 1024
CODE = 64


def aligned(index):
    return pl.ds(pl.multiple_of(index * BLOCK, BLOCK), BLOCK)


def score_tile(keys, query_rows):
    return lax.dot_general(keys, query_rows, NT, preferred_element_type=jnp.float32)


def for_groups(count, items, blocks_dev, body):
    def step(group, carry):
        slots = []
        for slot in range(GROUP):
            position = group * GROUP + slot
            code = items[jnp.minimum(position, count - 1)]
            unit = code // CODE
            slots.append(
                (
                    position,
                    position < count,
                    unit,
                    unit // blocks_dev,
                    unit % blocks_dev,
                    code % CODE,
                )
            )
        body(slots)
        return carry

    lax.fori_loop(0, (count + GROUP - 1) // GROUP, step, 0)


def text_kernel(
    blocks_dev,
    lists,
    lengths,
    q_in,
    text_in,
    near_items,
    far_items,
    counts,
    tops,
    totals,
    sums,
    q_ref,
    text,
    weights_all,
    sems,
):
    copies = [
        pltpu.make_async_copy(text_in, text, sems.at[0]),
        pltpu.make_async_copy(q_in, q_ref, sems.at[1]),
    ]
    for copy in copies:
        copy.start()
    base = lists[0, 0, 0]
    odd = (base // blocks_dev) % 2 == 1

    def plan_unit(unit, carry):
        head = unit // blocks_dev
        local = unit % blocks_dev

        def plan_entry(entry, carry):
            near, far = carry
            block = lists[head, local, entry] - base
            is_low = block < 0
            is_high = block >= blocks_dev
            is_outer = jnp.where(odd, is_high, is_low)
            is_inner = jnp.where(odd, is_low, is_high)
            shift = jnp.where(is_low, blocks_dev, jnp.where(is_high, -blocks_dev, 0))
            code = unit * CODE + block + shift

            @pl.when(is_outer)
            def _():
                far_items[far] = code

            @pl.when(jnp.logical_not(is_outer))
            def _():
                near_items[near] = code + jnp.where(is_inner, blocks_dev, 0)

            outer = is_outer.astype(jnp.int32)
            return near + 1 - outer, far + outer

        return lax.fori_loop(0, lengths[head, local], plan_entry, carry)

    zero = jnp.int32(0)
    near, far = lax.fori_loop(0, HEADS * blocks_dev, plan_unit, (zero, zero))
    counts[0] = near
    counts[1] = far
    for copy in copies:
        copy.wait()
    pairs = blocks_dev // 2

    def weights_head(head, carry):
        keys = text[0, :, aligned(head)]
        for pair in range(pairs):
            rows = pl.ds(pair * 2 * BLOCK, 2 * BLOCK)
            scores = score_tile(keys, q_ref[rows, aligned(head)])
            top = jnp.max(scores, axis=0, keepdims=True)
            weights = jnp.exp2((scores - top) * EXP2_SCALE)
            weights_all[head * pairs + pair] = weights.astype(jnp.bfloat16)
            total = jnp.sum(weights, axis=0, keepdims=True)
            for side in range(2):
                unit = head * blocks_dev + pair * 2 + side
                lanes = slice(side * BLOCK, (side + 1) * BLOCK)
                tops[unit] = top[:, lanes]
                totals[unit] = total[:, lanes]
        return carry

    lax.fori_loop(0, HEADS, weights_head, 0)

    def sums_head(head, carry):
        values_t = text[1, :, aligned(head)].T
        for pair in range(pairs):
            summed = jnp.dot(
                values_t, weights_all[head * pairs + pair], preferred_element_type=jnp.float32
            )
            for side in range(2):
                unit = head * blocks_dev + pair * 2 + side
                sums[unit] = summed[:, side * BLOCK : (side + 1) * BLOCK]
        return carry

    lax.fori_loop(0, HEADS, sums_head, 0)


def near_kernel(
    blocks_dev,
    near_items,
    counts,
    q_in,
    k_in,
    v_in,
    k_inner,
    v_inner,
    sums_in,
    text_tops,
    text_totals,
    tops,
    totals,
    sums,
    q_ref,
    k_ref,
    v_ref,
    vt_ref,
    scores_all,
    weights_all,
    sems,
):
    tokens = k_in.shape[0]
    first, second = pl.ds(0, tokens), pl.ds(tokens, tokens)
    moves = (
        (q_in, q_ref),
        (k_in, k_ref.at[first]),
        (k_inner, k_ref.at[second]),
        (v_in, v_ref.at[first]),
        (v_inner, v_ref.at[second]),
        (sums_in, sums),
    )
    copies = [
        pltpu.make_async_copy(source, target, sems.at[index])
        for index, (source, target) in enumerate(moves)
    ]
    for copy in copies:
        copy.start()
    count = counts[0]

    def turn(block, carry):
        for head in range(HEADS):
            lanes = slice(head * HEAD_DIM, (head + 1) * HEAD_DIM)
            vt_ref[lanes, aligned(block)] = v_ref[aligned(block), lanes].T
        return carry

    tops[...] = text_tops[...]
    for copy in copies[:3]:
        copy.wait()

    def top_body(slots):
        found = []
        for position, live, unit, head, local, block in slots:
            scores = score_tile(
                k_ref[aligned(block), aligned(head)], q_ref[aligned(local), aligned(head)]
            )
            scores_all[position] = scores
            found.append((unit, jnp.max(scores, axis=0, keepdims=True)))
        for unit, top in found:
            tops[unit] = jnp.maximum(tops[unit], top)

    for_groups(count, near_items, blocks_dev, top_body)
    factor = jnp.exp2((text_tops[...] - tops[...]) * EXP2_SCALE)
    totals[...] = text_totals[...] * factor
    copies[5].wait()
    sums[...] = sums[...] * factor

    def weights_body(slots):
        found = []
        for position, live, unit, head, local, block in slots:
            top = jnp.where(live, tops[unit], -NEVER)
            weights = jnp.exp2((scores_all[position] - top) * EXP2_SCALE)
            weights_all[position] = weights.astype(jnp.bfloat16)
            found.append((unit, jnp.sum(weights, axis=0, keepdims=True)))
        for unit, total in found:
            totals[unit] += total

    for_groups(count, near_items, blocks_dev, weights_body)

    def sum_body(slots):
        found = []
        for position, live, unit, head, local, block in slots:
            summed = jnp.dot(
                vt_ref[aligned(head), aligned(block)],
                weights_all[position],
                preferred_element_type=jnp.float32,
            )
            found.append((unit, summed))
        for unit, summed in found:
            sums[unit] += summed

    copies[3].wait()
    copies[4].wait()
    lax.fori_loop(0, 2 * blocks_dev, turn, 0)
    for_groups(count, near_items, blocks_dev, sum_body)


def middle_kernel(
    blocks_dev,
    far_items,
    counts,
    q_ref,
    k_far,
    near_tops,
    near_totals,
    sums,
    near_out,
    weights_out,
    tops,
    totals,
    levels,
    item_tops,
    item_totals,
    scores_all,
    weights_all,
    out_sems,
):
    tops[...] = near_tops[...]
    totals[...] = near_totals[...]
    count = counts[1]

    def total_body(slots):
        found = []
        for position, live, unit, head, local, block in slots:
            scores = score_tile(
                k_far[aligned(block), aligned(head)], q_ref[aligned(local), aligned(head)]
            )
            top = jnp.max(scores, axis=0, keepdims=True)
            total = jnp.sum(jnp.exp2((scores - top) * EXP2_SCALE), axis=0, keepdims=True)
            scores_all[position] = scores
            found.append((unit, position, jnp.where(live, top, NEVER), total))
        for unit, position, top, total in found:
            item_tops[position] = top
            item_totals[position] = total
            tops[unit] = jnp.maximum(tops[unit], top)

    for_groups(count, far_items, blocks_dev, total_body)
    totals[...] = totals[...] * jnp.exp2((near_tops[...] - tops[...]) * EXP2_SCALE)

    def fold_body(slots):
        found = []
        for position, live, unit, head, local, block in slots:
            add = jnp.exp2((item_tops[position] - tops[unit]) * EXP2_SCALE)
            found.append((unit, item_totals[position] * add))
        for unit, total in found:
            totals[unit] += total

    for_groups(count, far_items, blocks_dev, fold_body)
    levels[...] = tops[...] * EXP2_SCALE + jnp.log2(totals[...])

    def weights_body(slots):
        for position, live, unit, head, local, block in slots:
            level = jnp.where(live, levels[unit], -NEVER)
            weights = jnp.exp2(scores_all[position] * EXP2_SCALE - level).astype(jnp.bfloat16)
            weights_all[position] = weights.T
        first = pl.multiple_of(slots[0][0], GROUP)
        part = pl.ds(first, GROUP)
        pltpu.make_async_copy(
            weights_all.at[part], weights_out.at[part], out_sems.at[first // GROUP]
        ).start()

    for_groups(count, far_items, blocks_dev, weights_body)

    def near_rows(local, carry):
        for head in range(HEADS):
            unit = head * blocks_dev + local
            factor = jnp.exp2(near_tops[unit] * EXP2_SCALE - levels[unit])
            near_out[aligned(local), head * HEAD_DIM : (head + 1) * HEAD_DIM] = (
                sums[unit] * factor
            ).T
        return carry

    lax.fori_loop(0, blocks_dev, near_rows, 0)

    def settle(group, carry):
        part = pl.ds(pl.multiple_of(group * GROUP, GROUP), GROUP)
        pltpu.make_async_copy(weights_all.at[part], weights_out.at[part], out_sems.at[group]).wait()
        return carry

    lax.fori_loop(0, (count + GROUP - 1) // GROUP, settle, 0)


def last_kernel(
    blocks_dev,
    far_items,
    counts,
    near,
    weights,
    v_outer,
    out_ref,
    v_far,
    near_rows,
    total_rows,
    weights_all,
    sems,
    weight_sems,
):
    count = counts[1]
    groups = (count + GROUP - 1) // GROUP

    def weight_copy(group):
        part = pl.ds(pl.multiple_of(group * GROUP, GROUP), GROUP)
        return pltpu.make_async_copy(weights.at[part], weights_all.at[part], weight_sems.at[group])

    values_copy = pltpu.make_async_copy(v_outer, v_far, sems.at[0])
    near_copy = pltpu.make_async_copy(near, near_rows, sems.at[1])
    values_copy.start()

    def begin(group, carry):
        weight_copy(group).start()
        return carry

    lax.fori_loop(0, groups, begin, 0)
    near_copy.start()
    total_rows[...] = jnp.zeros(total_rows.shape, jnp.float32)
    values_copy.wait()

    def body(slots):
        weight_copy(slots[0][0] // GROUP).wait()
        parts = []
        for position, live, unit, head, local, block in slots:
            parts.append(
                jnp.dot(
                    weights_all[position],
                    v_far[aligned(block), aligned(head)],
                    preferred_element_type=jnp.float32,
                )
            )
        for slot, part in zip(slots, parts):
            total_rows[aligned(slot[4]), aligned(slot[3])] += part

    for_groups(count, far_items, blocks_dev, body)
    near_copy.wait()
    out_ref[...] = (total_rows[...] + near_rows[...]).astype(jnp.bfloat16)


def text_step(text, distances):
    count = lax.axis_size("seq")
    parts = [text]
    for distance in distances:
        parts.append(lax.ppermute(text, "seq", [(i, i ^ distance) for i in range(count)]))
    return jnp.concatenate(parts, axis=1)


def on_device(queries, video_keys, video_values, text_keys, text_values, block_lists, list_lengths):
    tokens = queries.shape[0]
    columns = queries.shape[1]
    blocks_dev = tokens // BLOCK
    count = lax.axis_size("seq")
    assert blocks_dev == REACH and 2 * blocks_dev <= CODE and count & (count - 1) == 0
    units = HEADS * blocks_dev
    longest = block_lists.shape[2]
    inner = [(i, i ^ 1) for i in range(count)]
    outer = [(i, i + 1) for i in range(1, count - 1, 2)]
    outer += [(target, source) for source, target in outer]

    smem = pl.BlockSpec(memory_space=pltpu.SMEM)
    vmem = pl.BlockSpec(memory_space=pltpu.VMEM)
    anywhere = pl.BlockSpec(memory_space=pl.ANY)
    stat = (units, 1, BLOCK)
    squares = (units, HEAD_DIM, BLOCK)
    room = -(-units * (longest - 1) // GROUP) * GROUP
    near_room = -(-units * longest // GROUP) * GROUP
    weights_shape = (room, BLOCK, BLOCK)
    near_shape = (near_room, BLOCK, BLOCK)
    params = pltpu.CompilerParams(vmem_limit_bytes=VMEM_BYTES)

    text = text_step(jnp.stack([text_keys, text_values], 0), (2,))
    keys, text = lax.optimization_barrier((video_keys, text))
    k_outer = lax.ppermute(keys, "seq", outer)
    k_inner = lax.ppermute(video_keys, "seq", inner)
    v_inner = lax.ppermute(video_values, "seq", inner)
    text = text_step(text, (4, 8, 12) if count >= 16 else (4,) if count == 8 else ())
    distance = 16
    while distance < count:
        text = text_step(text, (distance,))
        distance *= 2
    text = text_step(text, (1,))

    near_items, far_items, counts, text_tops, text_totals, text_sums = pl.pallas_call(
        functools.partial(text_kernel, blocks_dev),
        out_shape=(
            jax.ShapeDtypeStruct((near_room,), jnp.int32),
            jax.ShapeDtypeStruct((room,), jnp.int32),
            jax.ShapeDtypeStruct((2,), jnp.int32),
            jax.ShapeDtypeStruct(stat, jnp.float32),
            jax.ShapeDtypeStruct(stat, jnp.float32),
            jax.ShapeDtypeStruct(squares, jnp.float32),
        ),
        in_specs=[smem, smem, anywhere, anywhere],
        out_specs=(smem, smem, smem, vmem, vmem, vmem),
        scratch_shapes=[
            pltpu.VMEM((tokens, columns), jnp.bfloat16),
            pltpu.VMEM(text.shape, jnp.bfloat16),
            pltpu.VMEM((units // 2, text.shape[1], 2 * BLOCK), jnp.bfloat16),
            pltpu.SemaphoreType.DMA((2,)),
        ],
        compiler_params=params,
        cost_estimate=pl.CostEstimate(flops=1_000_000, bytes_accessed=10_000, transcendentals=0),
        name="text",
    )(block_lists, list_lengths, queries, text)

    values, near_items = lax.optimization_barrier((video_values, near_items))
    v_outer = lax.ppermute(values, "seq", outer)

    tops, totals, sums = pl.pallas_call(
        functools.partial(near_kernel, blocks_dev),
        out_shape=(
            jax.ShapeDtypeStruct(stat, jnp.float32),
            jax.ShapeDtypeStruct(stat, jnp.float32),
            jax.ShapeDtypeStruct(squares, jnp.float32),
        ),
        in_specs=[smem, smem] + [anywhere] * 6 + [vmem] * 2,
        out_specs=(vmem, vmem, vmem),
        scratch_shapes=[
            pltpu.VMEM((tokens, columns), jnp.bfloat16),
            pltpu.VMEM((2 * tokens, columns), jnp.bfloat16),
            pltpu.VMEM((2 * tokens, columns), jnp.bfloat16),
            pltpu.VMEM((columns, 2 * tokens), jnp.bfloat16),
            pltpu.VMEM(near_shape, jnp.float32),
            pltpu.VMEM(near_shape, jnp.bfloat16),
            pltpu.SemaphoreType.DMA((6,)),
        ],
        compiler_params=params,
        cost_estimate=pl.CostEstimate(flops=1_000_000, bytes_accessed=10_000, transcendentals=0),
        name="own",
    )(
        near_items,
        counts,
        queries,
        video_keys,
        video_values,
        k_inner,
        v_inner,
        text_sums,
        text_tops,
        text_totals,
    )

    near, weights = pl.pallas_call(
        functools.partial(middle_kernel, blocks_dev),
        out_shape=(
            jax.ShapeDtypeStruct((tokens, columns), jnp.float32),
            jax.ShapeDtypeStruct(weights_shape, jnp.bfloat16),
        ),
        in_specs=[smem, smem] + [vmem] * 5,
        out_specs=(vmem, anywhere),
        scratch_shapes=[
            pltpu.VMEM(stat, jnp.float32),
            pltpu.VMEM(stat, jnp.float32),
            pltpu.VMEM(stat, jnp.float32),
            pltpu.VMEM((room, 1, BLOCK), jnp.float32),
            pltpu.VMEM((room, 1, BLOCK), jnp.float32),
            pltpu.VMEM(weights_shape, jnp.float32),
            pltpu.VMEM(weights_shape, jnp.bfloat16),
            pltpu.SemaphoreType.DMA((room // GROUP,)),
        ],
        compiler_params=params,
        cost_estimate=pl.CostEstimate(
            flops=1_000_000, bytes_accessed=10_000, transcendentals=0
        ),
        name="middle",
    )(far_items, counts, queries, k_outer, tops, totals, sums)

    return pl.pallas_call(
        functools.partial(last_kernel, blocks_dev),
        out_shape=jax.ShapeDtypeStruct((tokens, columns), jnp.bfloat16),
        in_specs=[smem, smem] + [anywhere] * 3,
        out_specs=vmem,
        scratch_shapes=[
            pltpu.VMEM((tokens, columns), jnp.bfloat16),
            pltpu.VMEM((tokens, columns), jnp.float32),
            pltpu.VMEM((tokens, columns), jnp.float32),
            pltpu.VMEM(weights_shape, jnp.bfloat16),
            pltpu.SemaphoreType.DMA((2,)),
            pltpu.SemaphoreType.DMA((room // GROUP,)),
        ],
        compiler_params=params,
        cost_estimate=pl.CostEstimate(
            flops=1_000_000_000, bytes_accessed=9_000_000, transcendentals=0
        ),
        name="last",
    )(far_items, counts, near, weights, v_outer)


def solution(mesh):
    in_specs = (
        P(("groups", "seq"), None),
        P(("groups", "seq"), None),
        P(("groups", "seq"), None),
        P(("groups", "seq"), None),
        P(("groups", "seq"), None),
        P(None, ("groups", "seq"), None),
        P(None, ("groups", "seq")),
    )
    out_specs = P(("groups", "seq"), None)
    return jax.shard_map(
        on_device, mesh=mesh, in_specs=in_specs, out_specs=out_specs, check_vma=False
    )
```

```python
import functools
import math

import jax
import jax.numpy as jnp
from jax import lax
from jax.experimental import pallas as pl
from jax.experimental.pallas import tpu as pltpu
from jax.sharding import PartitionSpec as P

HEAD_DIM = 128
HEADS = 4
BLOCK = 128
REACH = 8
GROUP = 24
EXP2_SCALE = HEAD_DIM ** (-0.5) * math.log2(math.e)
NEVER = -1e30
NT = (((1,), (1,)), ((), ()))
VMEM_BYTES = 63 * 1024 * 1024
CODE = 64


def aligned(index):
    return pl.ds(pl.multiple_of(index * BLOCK, BLOCK), BLOCK)


def score_tile(keys, query_rows):
    return lax.dot_general(keys, query_rows, NT, preferred_element_type=jnp.float32)


def for_groups(first, count, items, blocks_dev, body):
    def step(group, carry):
        slots = []
        for slot in range(GROUP):
            position = group * GROUP + slot
            code = items[first + jnp.minimum(position, count - 1)]
            unit = code // CODE
            slots.append(
                (
                    position,
                    position < count,
                    unit,
                    unit // blocks_dev,
                    unit % blocks_dev,
                    code % CODE,
                )
            )
        body(slots)
        return carry

    lax.fori_loop(0, (count + GROUP - 1) // GROUP, step, 0)


def plan_items(blocks_dev, lists, lengths, near_items, far_items, counts):
    base = lists[0, 0, 0]
    odd = (base // blocks_dev) % 2 == 1

    def plan_unit(unit, carry):
        head = unit // blocks_dev
        local = unit % blocks_dev

        def plan_entry(entry, carry):
            near, far = carry
            block = lists[head, local, entry] - base
            is_low = block < 0
            is_high = block >= blocks_dev
            is_outer = jnp.where(odd, is_high, is_low)
            is_inner = jnp.where(odd, is_low, is_high)
            shift = jnp.where(is_low, blocks_dev, jnp.where(is_high, -blocks_dev, 0))
            code = unit * CODE + block + shift

            @pl.when(is_outer)
            def _():
                far_items[far] = code

            @pl.when(jnp.logical_not(is_outer))
            def _():
                near_items[near] = code + jnp.where(is_inner, blocks_dev, 0)

            outer = is_outer.astype(jnp.int32)
            return near + 1 - outer, far + outer

        return lax.fori_loop(0, lengths[head, local], plan_entry, carry)

    zero = jnp.int32(0)
    half = HEADS // 2 * blocks_dev
    split, far = lax.fori_loop(0, half, plan_unit, (zero, zero))
    near, far = lax.fori_loop(half, 2 * half, plan_unit, (split, far))
    counts[0] = zero
    counts[1] = split
    counts[2] = near
    counts[3] = far


def near_kernel(
    blocks_dev,
    half,
    near_items,
    counts,
    q_in,
    k_in,
    v_in,
    k_inner,
    v_inner,
    tops,
    totals,
    sums,
    q_ref,
    k_ref,
    v_ref,
    vt_ref,
    scores_all,
    weights_all,
    sems,
    prepare=None,
):
    tokens = k_in.shape[0]
    first_rows, second_rows = pl.ds(0, tokens), pl.ds(tokens, tokens)
    width = HEADS // 2 * HEAD_DIM
    lanes = pl.ds(half * width, width)
    moves = (
        (q_in.at[:, lanes], q_ref),
        (k_in.at[:, lanes], k_ref.at[first_rows]),
        (k_inner.at[:, lanes], k_ref.at[second_rows]),
        (v_in.at[:, lanes], v_ref.at[first_rows]),
        (v_inner.at[:, lanes], v_ref.at[second_rows]),
    )
    copies = [
        pltpu.make_async_copy(source, target, sems.at[index])
        for index, (source, target) in enumerate(moves)
    ]
    for copy in copies:
        copy.start()
    if prepare is not None:
        prepare()
    first = counts[half]
    count = counts[half + 1] - first

    def turn(block, carry):
        for head in range(HEADS // 2):
            lanes = slice(head * HEAD_DIM, (head + 1) * HEAD_DIM)
            vt_ref[lanes, aligned(block)] = v_ref[aligned(block), lanes].T
        return carry

    tops[...] = jnp.full(tops.shape, NEVER, jnp.float32)
    totals[...] = jnp.zeros(totals.shape, jnp.float32)
    sums[...] = jnp.zeros(sums.shape, jnp.float32)
    for copy in copies[:3]:
        copy.wait()

    def top_body(slots):
        found = []
        for position, live, unit, head, local, block in slots:
            unit, head = unit - half * HEADS // 2 * blocks_dev, head - half * HEADS // 2
            scores = score_tile(
                k_ref[aligned(block), aligned(head)], q_ref[aligned(local), aligned(head)]
            )
            scores_all[position] = scores
            found.append((unit, jnp.max(scores, axis=0, keepdims=True)))
        for unit, top in found:
            tops[unit] = jnp.maximum(tops[unit], top)

    for_groups(first, count, near_items, blocks_dev, top_body)

    def weights_body(slots):
        found = []
        for position, live, unit, head, local, block in slots:
            unit, head = unit - half * HEADS // 2 * blocks_dev, head - half * HEADS // 2
            top = jnp.where(live, tops[unit], -NEVER)
            weights = jnp.exp2((scores_all[position] - top) * EXP2_SCALE)
            weights_all[position] = weights.astype(jnp.bfloat16)
            found.append((unit, jnp.sum(weights, axis=0, keepdims=True)))
        for unit, total in found:
            totals[unit] += total

    for_groups(first, count, near_items, blocks_dev, weights_body)

    def sum_body(slots):
        found = []
        for position, live, unit, head, local, block in slots:
            unit, head = unit - half * HEADS // 2 * blocks_dev, head - half * HEADS // 2
            summed = jnp.dot(
                vt_ref[aligned(head), aligned(block)],
                weights_all[position],
                preferred_element_type=jnp.float32,
            )
            found.append((unit, summed))
        for unit, summed in found:
            sums[unit] += summed

    copies[3].wait()
    copies[4].wait()
    lax.fori_loop(0, 2 * blocks_dev, turn, 0)
    for_groups(first, count, near_items, blocks_dev, sum_body)


def first_kernel(blocks_dev, lists, lengths, *refs):
    inputs, (near_items, far_items, counts), value_halves = refs[:5], refs[5:8], refs[8:10]
    others, (held, half_sems) = refs[10:-2], refs[-2:]
    values = inputs[2]
    width = values.shape[1] // 2
    loads = [
        pltpu.make_async_copy(
            values.at[:, pl.ds(side * width, width)], held.at[side], half_sems.at[side]
        )
        for side in range(2)
    ]
    stores = [
        pltpu.make_async_copy(held.at[side], value_halves[side], half_sems.at[2 + side])
        for side in range(2)
    ]

    def prepare():
        plan_items(blocks_dev, lists, lengths, near_items, far_items, counts)
        for load, store in zip(loads, stores):
            load.wait()
            store.start()

    for load in loads:
        load.start()
    near_kernel(blocks_dev, 0, near_items, counts, *inputs, *others, prepare=prepare)
    for store in stores:
        store.wait()


def middle_kernel(
    blocks_dev,
    far_items,
    counts,
    q_ref,
    k_far,
    *refs,
):
    parts, refs = refs[: -24], refs[-24 :]
    (
        tops_a,
        totals_a,
        sums_a,
        tops_b,
        totals_b,
        sums_b,
        near_out,
        weights_out,
        tops,
        totals,
        levels,
        text_tops,
        text_totals,
        text_sums,
        text_weights,
        near_tops,
        near_totals,
        item_tops,
        item_totals,
        scores_all,
        weights_all,
        out_sems,
        text,
        text_sems,
    ) = refs
    rows = parts[0].shape[1]
    copies = [
        pltpu.make_async_copy(
            part, text.at[:, pl.ds(index * rows, rows)], text_sems.at[index]
        )
        for index, part in enumerate(parts)
    ]
    for copy in copies:
        copy.start()
    half = HEADS // 2 * blocks_dev
    near_tops[:half] = tops_a[...]
    near_tops[half:] = tops_b[...]
    near_totals[:half] = totals_a[...]
    near_totals[half:] = totals_b[...]
    tops[...] = near_tops[...]
    count = counts[3]

    def total_body(slots):
        found = []
        for position, live, unit, head, local, block in slots:
            scores = score_tile(
                k_far[aligned(block), aligned(head)], q_ref[aligned(local), aligned(head)]
            )
            top = jnp.max(scores, axis=0, keepdims=True)
            total = jnp.sum(jnp.exp2((scores - top) * EXP2_SCALE), axis=0, keepdims=True)
            scores_all[position] = scores
            found.append((unit, position, jnp.where(live, top, NEVER), total))
        for unit, position, top, total in found:
            item_tops[position] = top
            item_totals[position] = total
            tops[unit] = jnp.maximum(tops[unit], top)

    for_groups(0, count, far_items, blocks_dev, total_body)
    for copy in copies:
        copy.wait()
    pairs = blocks_dev // 2

    def text_weights_head(head, carry):
        keys = text[0, :, aligned(head)]
        for pair in range(pairs):
            rows = pl.ds(pair * 2 * BLOCK, 2 * BLOCK)
            scores = score_tile(keys, q_ref[rows, aligned(head)])
            top = jnp.max(scores, axis=0, keepdims=True)
            weights = jnp.exp2((scores - top) * EXP2_SCALE)
            text_weights[head * pairs + pair] = weights.astype(jnp.bfloat16)
            total = jnp.sum(weights, axis=0, keepdims=True)
            for side in range(2):
                unit = head * blocks_dev + pair * 2 + side
                lanes = slice(side * BLOCK, (side + 1) * BLOCK)
                text_tops[unit] = top[:, lanes]
                text_totals[unit] = total[:, lanes]
        return carry

    lax.fori_loop(0, HEADS, text_weights_head, 0)

    def text_sums_head(head, carry):
        values_t = text[1, :, aligned(head)].T
        for pair in range(pairs):
            summed = jnp.dot(
                values_t, text_weights[head * pairs + pair], preferred_element_type=jnp.float32
            )
            for side in range(2):
                unit = head * blocks_dev + pair * 2 + side
                text_sums[unit] = summed[:, side * BLOCK : (side + 1) * BLOCK]
        return carry

    lax.fori_loop(0, HEADS, text_sums_head, 0)
    tops[...] = jnp.maximum(tops[...], text_tops[...])
    near_share = near_totals[...] * jnp.exp2((near_tops[...] - tops[...]) * EXP2_SCALE)
    text_share = text_totals[...] * jnp.exp2((text_tops[...] - tops[...]) * EXP2_SCALE)
    totals[...] = near_share + text_share

    def fold_body(slots):
        found = []
        for position, live, unit, head, local, block in slots:
            add = jnp.exp2((item_tops[position] - tops[unit]) * EXP2_SCALE)
            found.append((unit, item_totals[position] * add))
        for unit, total in found:
            totals[unit] += total

    for_groups(0, count, far_items, blocks_dev, fold_body)
    levels[...] = tops[...] * EXP2_SCALE + jnp.log2(totals[...])

    def weights_body(slots):
        for position, live, unit, head, local, block in slots:
            level = jnp.where(live, levels[unit], -NEVER)
            weights = jnp.exp2(scores_all[position] * EXP2_SCALE - level).astype(jnp.bfloat16)
            weights_all[position] = weights.T
        first = pl.multiple_of(slots[0][0], GROUP)
        part = pl.ds(first, GROUP)
        pltpu.make_async_copy(
            weights_all.at[part], weights_out.at[part], out_sems.at[first // GROUP]
        ).start()

    for_groups(0, count, far_items, blocks_dev, weights_body)

    def near_rows(local, carry):
        for head in range(HEADS):
            unit = head * blocks_dev + local
            sums = sums_a if head < HEADS // 2 else sums_b
            near_factor = jnp.exp2(near_tops[unit] * EXP2_SCALE - levels[unit])
            text_factor = jnp.exp2(text_tops[unit] * EXP2_SCALE - levels[unit])
            near_out[aligned(local), head * HEAD_DIM : (head + 1) * HEAD_DIM] = (
                sums[head % (HEADS // 2) * blocks_dev + local] * near_factor
                + text_sums[unit] * text_factor
            ).T
        return carry

    lax.fori_loop(0, blocks_dev, near_rows, 0)

    def settle(group, carry):
        part = pl.ds(pl.multiple_of(group * GROUP, GROUP), GROUP)
        pltpu.make_async_copy(weights_all.at[part], weights_out.at[part], out_sems.at[group]).wait()
        return carry

    lax.fori_loop(0, (count + GROUP - 1) // GROUP, settle, 0)


def last_kernel(
    blocks_dev,
    far_items,
    counts,
    near,
    weights,
    v_left,
    v_right,
    out_ref,
    v_far,
    near_rows,
    total_rows,
    weights_all,
    sems,
    weight_sems,
):
    count = counts[3]
    groups = (count + GROUP - 1) // GROUP

    def weight_copy(group):
        part = pl.ds(pl.multiple_of(group * GROUP, GROUP), GROUP)
        return pltpu.make_async_copy(weights.at[part], weights_all.at[part], weight_sems.at[group])

    width = v_left.shape[1]
    values_copies = [
        pltpu.make_async_copy(half, v_far.at[:, pl.ds(side * width, width)], sems.at[side])
        for side, half in enumerate((v_left, v_right))
    ]
    near_copy = pltpu.make_async_copy(near, near_rows, sems.at[2])
    for copy in values_copies:
        copy.start()

    def begin(group, carry):
        weight_copy(group).start()
        return carry

    lax.fori_loop(0, groups, begin, 0)
    near_copy.start()
    total_rows[...] = jnp.zeros(total_rows.shape, jnp.float32)
    for copy in values_copies:
        copy.wait()

    def body(slots):
        weight_copy(slots[0][0] // GROUP).wait()
        parts = []
        for position, live, unit, head, local, block in slots:
            parts.append(
                jnp.dot(
                    weights_all[position],
                    v_far[aligned(block), aligned(head)],
                    preferred_element_type=jnp.float32,
                )
            )
        for slot, part in zip(slots, parts):
            total_rows[aligned(slot[4]), aligned(slot[3])] += part

    for_groups(0, count, far_items, blocks_dev, body)
    near_copy.wait()
    out_ref[...] = (total_rows[...] + near_rows[...]).astype(jnp.bfloat16)


def text_parts(text, distances):
    count = lax.axis_size("seq")
    parts = [text]
    for distance in distances:
        parts.append(lax.ppermute(text, "seq", [(i, i ^ distance) for i in range(count)]))
    return parts


def text_step(text, distances):
    return jnp.concatenate(text_parts(text, distances), axis=1)


def on_device(queries, video_keys, video_values, text_keys, text_values, block_lists, list_lengths):
    tokens = queries.shape[0]
    columns = queries.shape[1]
    blocks_dev = tokens // BLOCK
    count = lax.axis_size("seq")
    assert blocks_dev == REACH and 2 * blocks_dev <= CODE and count & (count - 1) == 0
    units = HEADS * blocks_dev
    longest = block_lists.shape[2]
    inner = [(i, i ^ 1) for i in range(count)]
    outer = [(i, i + 1) for i in range(1, count - 1, 2)]
    outer += [(target, source) for source, target in outer]

    smem = pl.BlockSpec(memory_space=pltpu.SMEM)
    vmem = pl.BlockSpec(memory_space=pltpu.VMEM)
    anywhere = pl.BlockSpec(memory_space=pl.ANY)
    stat = (units, 1, BLOCK)
    squares = (units, HEAD_DIM, BLOCK)
    room = -(-units * (longest - 1) // GROUP) * GROUP
    near_room = -(-units * longest // GROUP) * GROUP
    weights_shape = (room, BLOCK, BLOCK)
    near_shape = (-(-units // 2 * longest // GROUP) * GROUP, BLOCK, BLOCK)
    half_stat = (units // 2, 1, BLOCK)
    half_squares = (units // 2, HEAD_DIM, BLOCK)
    params = pltpu.CompilerParams(vmem_limit_bytes=VMEM_BYTES)

    text = text_step(jnp.stack([text_keys, text_values], 0), (2,))
    keys, text = lax.optimization_barrier((video_keys, text))
    k_outer = lax.ppermute(keys, "seq", outer)
    k_inner = lax.ppermute(keys, "seq", inner)
    v_inner = lax.ppermute(video_values, "seq", inner)
    text = text_step(text, (1,))
    distance = 16
    while distance < count:
        text = text_step(text, (distance,))
        distance *= 2
    text, k_inner = lax.optimization_barrier((text, k_inner))
    item_shapes = (
        jax.ShapeDtypeStruct((near_room,), jnp.int32),
        jax.ShapeDtypeStruct((room,), jnp.int32),
        jax.ShapeDtypeStruct((4,), jnp.int32),
    )
    near_scratch = [
        pltpu.VMEM((tokens, columns // 2), jnp.bfloat16),
        pltpu.VMEM((2 * tokens, columns // 2), jnp.bfloat16),
        pltpu.VMEM((2 * tokens, columns // 2), jnp.bfloat16),
        pltpu.VMEM((columns // 2, 2 * tokens), jnp.bfloat16),
        pltpu.VMEM(near_shape, jnp.float32),
        pltpu.VMEM(near_shape, jnp.bfloat16),
        pltpu.SemaphoreType.DMA((5,)),
    ]
    near_params = dict(
        in_specs=[smem, smem] + [anywhere] * 5,
        compiler_params=params,
        cost_estimate=pl.CostEstimate(flops=1_000_000, bytes_accessed=10_000, transcendentals=0),
    )
    near_shapes = (
        jax.ShapeDtypeStruct(half_stat, jnp.float32),
        jax.ShapeDtypeStruct(half_stat, jnp.float32),
        jax.ShapeDtypeStruct(half_squares, jnp.float32),
    )
    half_values = jax.ShapeDtypeStruct((tokens, columns // 2), jnp.bfloat16)
    near_inputs = (queries, video_keys, video_values, k_inner, v_inner)
    near_items, far_items, counts, left, right, tops_a, totals_a, sums_a = pl.pallas_call(
        functools.partial(first_kernel, blocks_dev),
        out_shape=item_shapes + (half_values, half_values) + near_shapes,
        out_specs=(smem, smem, smem, anywhere, anywhere, vmem, vmem, vmem),
        scratch_shapes=near_scratch
        + [pltpu.VMEM((2, tokens, columns // 2), jnp.bfloat16), pltpu.SemaphoreType.DMA((4,))],
        name="near_first",
        **near_params,
    )(block_lists, list_lengths, *near_inputs)
    v_left = lax.ppermute(left, "seq", outer)
    tops_b, totals_b, sums_b = pl.pallas_call(
        functools.partial(near_kernel, blocks_dev, 1),
        out_shape=near_shapes,
        out_specs=(vmem, vmem, vmem),
        scratch_shapes=near_scratch,
        name="near_second",
        **near_params,
    )(near_items, counts, *near_inputs)
    parts = text_parts(text, (4, 8, 12) if count >= 16 else (4,) if count == 8 else ())
    *parts, tops_b = lax.optimization_barrier((*parts, tops_b))
    right, k_outer, *parts = lax.optimization_barrier((right, k_outer, *parts))
    v_right = lax.ppermute(right, "seq", outer)

    text_rows = text_keys.shape[0] * count
    near, weights = pl.pallas_call(
        functools.partial(middle_kernel, blocks_dev),
        out_shape=(
            jax.ShapeDtypeStruct((tokens, columns), jnp.float32),
            jax.ShapeDtypeStruct(weights_shape, jnp.bfloat16),
        ),
        in_specs=[smem, smem, vmem, vmem] + [anywhere] * len(parts) + [vmem] * 6,
        out_specs=(vmem, anywhere),
        scratch_shapes=[
            pltpu.VMEM(stat, jnp.float32),
            pltpu.VMEM(stat, jnp.float32),
            pltpu.VMEM(stat, jnp.float32),
            pltpu.VMEM(stat, jnp.float32),
            pltpu.VMEM(stat, jnp.float32),
            pltpu.VMEM(squares, jnp.float32),
            pltpu.VMEM((units // 2, text_rows, 2 * BLOCK), jnp.bfloat16),
            pltpu.VMEM(stat, jnp.float32),
            pltpu.VMEM(stat, jnp.float32),
            pltpu.VMEM((room, 1, BLOCK), jnp.float32),
            pltpu.VMEM((room, 1, BLOCK), jnp.float32),
            pltpu.VMEM(weights_shape, jnp.float32),
            pltpu.VMEM(weights_shape, jnp.bfloat16),
            pltpu.SemaphoreType.DMA((room // GROUP,)),
            pltpu.VMEM((2, text_rows, columns), jnp.bfloat16),
            pltpu.SemaphoreType.DMA((len(parts),)),
        ],
        compiler_params=params,
        cost_estimate=pl.CostEstimate(
            flops=1_000_000, bytes_accessed=10_000, transcendentals=0
        ),
        name="middle",
    )(
        far_items,
        counts,
        queries,
        k_outer,
        *parts,
        tops_a,
        totals_a,
        sums_a,
        tops_b,
        totals_b,
        sums_b,
    )

    return pl.pallas_call(
        functools.partial(last_kernel, blocks_dev),
        out_shape=jax.ShapeDtypeStruct((tokens, columns), jnp.bfloat16),
        in_specs=[smem, smem] + [anywhere] * 4,
        out_specs=vmem,
        scratch_shapes=[
            pltpu.VMEM((tokens, columns), jnp.bfloat16),
            pltpu.VMEM((tokens, columns), jnp.float32),
            pltpu.VMEM((tokens, columns), jnp.float32),
            pltpu.VMEM(weights_shape, jnp.bfloat16),
            pltpu.SemaphoreType.DMA((3,)),
            pltpu.SemaphoreType.DMA((room // GROUP,)),
        ],
        compiler_params=params,
        cost_estimate=pl.CostEstimate(
            flops=1_000_000_000, bytes_accessed=9_000_000, transcendentals=0
        ),
        name="last",
    )(far_items, counts, near, weights, v_left, v_right)


def solution(mesh):
    in_specs = (
        P(("groups", "seq"), None),
        P(("groups", "seq"), None),
        P(("groups", "seq"), None),
        P(("groups", "seq"), None),
        P(("groups", "seq"), None),
        P(None, ("groups", "seq"), None),
        P(None, ("groups", "seq")),
    )
    out_specs = P(("groups", "seq"), None)
    return jax.shard_map(
        on_device, mesh=mesh, in_specs=in_specs, out_specs=out_specs, check_vma=False
    )
```

```python
import functools
import math

import jax
import jax.numpy as jnp
from jax import lax
from jax.experimental import pallas as pl
from jax.experimental.pallas import tpu as pltpu
from jax.sharding import PartitionSpec as P

HEAD_DIM = 128
HEADS = 4
BLOCK = 128
REACH = 8
GROUP = 24
EXP2_SCALE = HEAD_DIM ** (-0.5) * math.log2(math.e)
NEVER = -1e30
NT = (((1,), (1,)), ((), ()))
VMEM_BYTES = 63 * 1024 * 1024
CODE = 64


def aligned(index):
    return pl.ds(pl.multiple_of(index * BLOCK, BLOCK), BLOCK)


def score_tile(keys, query_rows):
    return lax.dot_general(keys, query_rows, NT, preferred_element_type=jnp.float32)


def for_groups(first, count, items, blocks_dev, body):
    def step(group, carry):
        slots = []
        for slot in range(GROUP):
            position = group * GROUP + slot
            code = items[first + jnp.minimum(position, count - 1)]
            unit = code // CODE
            slots.append(
                (
                    position,
                    position < count,
                    unit,
                    unit // blocks_dev,
                    unit % blocks_dev,
                    code % CODE,
                )
            )
        body(slots)
        return carry

    lax.fori_loop(0, (count + GROUP - 1) // GROUP, step, 0)


def plan_items(blocks_dev, lists, lengths, near_items, far_items, counts):
    base = lists[0, 0, 0]
    odd = (base // blocks_dev) % 2 == 1

    def plan_unit(unit, carry):
        head = unit // blocks_dev
        local = unit % blocks_dev

        def plan_entry(entry, carry):
            near, far = carry
            block = lists[head, local, entry] - base
            is_low = block < 0
            is_high = block >= blocks_dev
            is_outer = jnp.where(odd, is_high, is_low)
            is_inner = jnp.where(odd, is_low, is_high)
            shift = jnp.where(is_low, blocks_dev, jnp.where(is_high, -blocks_dev, 0))
            code = unit * CODE + block + shift

            @pl.when(is_outer)
            def _():
                far_items[far] = code

            @pl.when(jnp.logical_not(is_outer))
            def _():
                near_items[near] = code + jnp.where(is_inner, blocks_dev, 0)

            outer = is_outer.astype(jnp.int32)
            return near + 1 - outer, far + outer

        return lax.fori_loop(0, lengths[head, local], plan_entry, carry)

    zero = jnp.int32(0)
    half = HEADS // 2 * blocks_dev
    split, far = lax.fori_loop(0, half, plan_unit, (zero, zero))
    near, far = lax.fori_loop(half, 2 * half, plan_unit, (split, far))
    counts[0] = zero
    counts[1] = split
    counts[2] = near
    counts[3] = far


def near_kernel(
    blocks_dev,
    half,
    near_items,
    counts,
    q_in,
    k_in,
    v_in,
    k_inner,
    v_inner,
    tops,
    totals,
    sums,
    q_ref,
    k_ref,
    v_ref,
    vt_ref,
    scores_all,
    weights_all,
    sems,
    prepare=None,
):
    tokens = k_in.shape[0]
    first_rows, second_rows = pl.ds(0, tokens), pl.ds(tokens, tokens)
    width = HEADS // 2 * HEAD_DIM
    lanes = pl.ds(half * width, width)
    moves = (
        (q_in.at[:, lanes], q_ref),
        (k_in.at[:, lanes], k_ref.at[first_rows]),
        (k_inner.at[:, lanes], k_ref.at[second_rows]),
        (v_in.at[:, lanes], v_ref.at[first_rows]),
        (v_inner.at[:, lanes], v_ref.at[second_rows]),
    )
    copies = [
        pltpu.make_async_copy(source, target, sems.at[index])
        for index, (source, target) in enumerate(moves)
    ]
    for copy in copies:
        copy.start()
    if prepare is not None:
        prepare()
    first = counts[half]
    count = counts[half + 1] - first

    def turn(block, carry):
        for head in range(HEADS // 2):
            lanes = slice(head * HEAD_DIM, (head + 1) * HEAD_DIM)
            vt_ref[lanes, aligned(block)] = v_ref[aligned(block), lanes].T
        return carry

    tops[...] = jnp.full(tops.shape, NEVER, jnp.float32)
    totals[...] = jnp.zeros(totals.shape, jnp.float32)
    sums[...] = jnp.zeros(sums.shape, jnp.float32)
    for copy in copies[:3]:
        copy.wait()

    def top_body(slots):
        found = []
        for position, live, unit, head, local, block in slots:
            unit, head = unit - half * HEADS // 2 * blocks_dev, head - half * HEADS // 2
            scores = score_tile(
                k_ref[aligned(block), aligned(head)], q_ref[aligned(local), aligned(head)]
            )
            scores_all[position] = scores
            found.append((unit, jnp.max(scores, axis=0, keepdims=True)))
        for unit, top in found:
            tops[unit] = jnp.maximum(tops[unit], top)

    for_groups(first, count, near_items, blocks_dev, top_body)

    def weights_body(slots):
        found = []
        for position, live, unit, head, local, block in slots:
            unit, head = unit - half * HEADS // 2 * blocks_dev, head - half * HEADS // 2
            top = jnp.where(live, tops[unit], -NEVER)
            weights = jnp.exp2((scores_all[position] - top) * EXP2_SCALE)
            weights_all[position] = weights.astype(jnp.bfloat16)
            found.append((unit, jnp.sum(weights, axis=0, keepdims=True)))
        for unit, total in found:
            totals[unit] += total

    for_groups(first, count, near_items, blocks_dev, weights_body)

    def sum_body(slots):
        found = []
        for position, live, unit, head, local, block in slots:
            unit, head = unit - half * HEADS // 2 * blocks_dev, head - half * HEADS // 2
            summed = jnp.dot(
                vt_ref[aligned(head), aligned(block)],
                weights_all[position],
                preferred_element_type=jnp.float32,
            )
            found.append((unit, summed))
        for unit, summed in found:
            sums[unit] += summed

    copies[3].wait()
    copies[4].wait()
    lax.fori_loop(0, 2 * blocks_dev, turn, 0)
    for_groups(first, count, near_items, blocks_dev, sum_body)


def first_kernel(blocks_dev, lists, lengths, *refs):
    inputs, (near_items, far_items, counts), value_halves = refs[:5], refs[5:8], refs[8:10]
    others, (held, half_sems) = refs[10:-2], refs[-2:]
    values = inputs[2]
    width = values.shape[1] // 2
    loads = [
        pltpu.make_async_copy(
            values.at[:, pl.ds(side * width, width)], held.at[side], half_sems.at[side]
        )
        for side in range(2)
    ]
    stores = [
        pltpu.make_async_copy(held.at[side], value_halves[side], half_sems.at[2 + side])
        for side in range(2)
    ]

    def prepare():
        plan_items(blocks_dev, lists, lengths, near_items, far_items, counts)
        for load, store in zip(loads, stores):
            load.wait()
            store.start()

    for load in loads:
        load.start()
    near_kernel(blocks_dev, 0, near_items, counts, *inputs, *others, prepare=prepare)
    for store in stores:
        store.wait()


def middle_kernel(
    blocks_dev,
    far_items,
    counts,
    q_ref,
    k_far,
    *refs,
):
    parts, refs = refs[:-26], refs[-26:]
    (
        tops_a,
        totals_a,
        sums_a,
        tops_b,
        totals_b,
        sums_b,
        near_out,
        weights_out,
        tops,
        totals,
        levels,
        text_tops,
        text_totals,
        text_sums,
        text_weights,
        near_tops,
        near_totals,
        item_tops,
        item_totals,
        scores_all,
        weights_all,
        out_sems,
        text,
        text_sems,
        sums_all,
        sums_sems,
    ) = refs
    rows = parts[0].shape[1]
    copies = [
        pltpu.make_async_copy(
            part, text.at[:, pl.ds(index * rows, rows)], text_sems.at[index]
        )
        for index, part in enumerate(parts)
    ]
    sums_copies = [
        pltpu.make_async_copy(source, sums_all.at[side], sums_sems.at[side])
        for side, source in enumerate((sums_a, sums_b))
    ]
    for copy in copies + sums_copies:
        copy.start()
    half = HEADS // 2 * blocks_dev
    near_tops[:half] = tops_a[...]
    near_tops[half:] = tops_b[...]
    near_totals[:half] = totals_a[...]
    near_totals[half:] = totals_b[...]
    tops[...] = near_tops[...]
    count = counts[3]

    def total_body(slots):
        found = []
        for position, live, unit, head, local, block in slots:
            scores = score_tile(
                k_far[aligned(block), aligned(head)], q_ref[aligned(local), aligned(head)]
            )
            top = jnp.max(scores, axis=0, keepdims=True)
            total = jnp.sum(jnp.exp2((scores - top) * EXP2_SCALE), axis=0, keepdims=True)
            scores_all[position] = scores
            found.append((unit, position, jnp.where(live, top, NEVER), total))
        for unit, position, top, total in found:
            item_tops[position] = top
            item_totals[position] = total
            tops[unit] = jnp.maximum(tops[unit], top)

    for_groups(0, count, far_items, blocks_dev, total_body)
    for copy in copies:
        copy.wait()
    pairs = blocks_dev // 2

    def text_weights_head(head, carry):
        keys = text[0, :, aligned(head)]
        for pair in range(pairs):
            rows = pl.ds(pair * 2 * BLOCK, 2 * BLOCK)
            scores = score_tile(keys, q_ref[rows, aligned(head)])
            top = jnp.max(scores, axis=0, keepdims=True)
            weights = jnp.exp2((scores - top) * EXP2_SCALE)
            text_weights[head * pairs + pair] = weights.astype(jnp.bfloat16)
            total = jnp.sum(weights, axis=0, keepdims=True)
            for side in range(2):
                unit = head * blocks_dev + pair * 2 + side
                lanes = slice(side * BLOCK, (side + 1) * BLOCK)
                text_tops[unit] = top[:, lanes]
                text_totals[unit] = total[:, lanes]
        return carry

    lax.fori_loop(0, HEADS, text_weights_head, 0)

    def text_sums_head(head, carry):
        values_t = text[1, :, aligned(head)].T
        for pair in range(pairs):
            summed = jnp.dot(
                values_t, text_weights[head * pairs + pair], preferred_element_type=jnp.float32
            )
            for side in range(2):
                unit = head * blocks_dev + pair * 2 + side
                text_sums[unit] = summed[:, side * BLOCK : (side + 1) * BLOCK]
        return carry

    lax.fori_loop(0, HEADS, text_sums_head, 0)
    tops[...] = jnp.maximum(tops[...], text_tops[...])
    near_share = near_totals[...] * jnp.exp2((near_tops[...] - tops[...]) * EXP2_SCALE)
    text_share = text_totals[...] * jnp.exp2((text_tops[...] - tops[...]) * EXP2_SCALE)
    totals[...] = near_share + text_share

    def fold_body(slots):
        found = []
        for position, live, unit, head, local, block in slots:
            add = jnp.exp2((item_tops[position] - tops[unit]) * EXP2_SCALE)
            found.append((unit, item_totals[position] * add))
        for unit, total in found:
            totals[unit] += total

    for_groups(0, count, far_items, blocks_dev, fold_body)
    levels[...] = tops[...] * EXP2_SCALE + jnp.log2(totals[...])

    def weights_body(slots):
        for position, live, unit, head, local, block in slots:
            level = jnp.where(live, levels[unit], -NEVER)
            weights = jnp.exp2(scores_all[position] * EXP2_SCALE - level).astype(jnp.bfloat16)
            weights_all[position] = weights.T
        first = pl.multiple_of(slots[0][0], GROUP)
        part = pl.ds(first, GROUP)
        pltpu.make_async_copy(
            weights_all.at[part], weights_out.at[part], out_sems.at[first // GROUP]
        ).start()

    for_groups(0, count, far_items, blocks_dev, weights_body)

    for copy in sums_copies:
        copy.wait()

    def near_rows(local, carry):
        for head in range(HEADS):
            unit = head * blocks_dev + local
            sums = sums_all.at[head // (HEADS // 2)]
            near_factor = jnp.exp2(near_tops[unit] * EXP2_SCALE - levels[unit])
            text_factor = jnp.exp2(text_tops[unit] * EXP2_SCALE - levels[unit])
            near_out[aligned(local), head * HEAD_DIM : (head + 1) * HEAD_DIM] = (
                sums[head % (HEADS // 2) * blocks_dev + local] * near_factor
                + text_sums[unit] * text_factor
            ).T
        return carry

    lax.fori_loop(0, blocks_dev, near_rows, 0)

    def settle(group, carry):
        part = pl.ds(pl.multiple_of(group * GROUP, GROUP), GROUP)
        pltpu.make_async_copy(weights_all.at[part], weights_out.at[part], out_sems.at[group]).wait()
        return carry

    lax.fori_loop(0, (count + GROUP - 1) // GROUP, settle, 0)


def last_kernel(
    blocks_dev,
    far_items,
    counts,
    near,
    weights,
    v_left,
    v_right,
    out_ref,
    v_far,
    near_rows,
    total_rows,
    weights_all,
    sems,
    weight_sems,
):
    count = counts[3]
    groups = (count + GROUP - 1) // GROUP

    def weight_copy(group):
        part = pl.ds(pl.multiple_of(group * GROUP, GROUP), GROUP)
        return pltpu.make_async_copy(weights.at[part], weights_all.at[part], weight_sems.at[group])

    width = v_left.shape[1]
    values_copies = [
        pltpu.make_async_copy(half, v_far.at[:, pl.ds(side * width, width)], sems.at[side])
        for side, half in enumerate((v_left, v_right))
    ]
    near_copy = pltpu.make_async_copy(near, near_rows, sems.at[2])
    for copy in values_copies:
        copy.start()

    def begin(group, carry):
        weight_copy(group).start()
        return carry

    lax.fori_loop(0, groups, begin, 0)
    near_copy.start()
    total_rows[...] = jnp.zeros(total_rows.shape, jnp.float32)
    for copy in values_copies:
        copy.wait()

    def body(slots):
        weight_copy(slots[0][0] // GROUP).wait()
        parts = []
        for position, live, unit, head, local, block in slots:
            parts.append(
                jnp.dot(
                    weights_all[position],
                    v_far[aligned(block), aligned(head)],
                    preferred_element_type=jnp.float32,
                )
            )
        for slot, part in zip(slots, parts):
            total_rows[aligned(slot[4]), aligned(slot[3])] += part

    for_groups(0, count, far_items, blocks_dev, body)
    near_copy.wait()
    out_ref[...] = (total_rows[...] + near_rows[...]).astype(jnp.bfloat16)


def text_parts(text, distances):
    count = lax.axis_size("seq")
    parts = [text]
    for distance in distances:
        parts.append(lax.ppermute(text, "seq", [(i, i ^ distance) for i in range(count)]))
    return parts


def text_step(text, distances):
    return jnp.concatenate(text_parts(text, distances), axis=1)


def on_device(queries, video_keys, video_values, text_keys, text_values, block_lists, list_lengths):
    tokens = queries.shape[0]
    columns = queries.shape[1]
    blocks_dev = tokens // BLOCK
    count = lax.axis_size("seq")
    assert blocks_dev == REACH and 2 * blocks_dev <= CODE and count & (count - 1) == 0
    units = HEADS * blocks_dev
    longest = block_lists.shape[2]
    inner = [(i, i ^ 1) for i in range(count)]
    outer = [(i, i + 1) for i in range(1, count - 1, 2)]
    outer += [(target, source) for source, target in outer]

    smem = pl.BlockSpec(memory_space=pltpu.SMEM)
    vmem = pl.BlockSpec(memory_space=pltpu.VMEM)
    anywhere = pl.BlockSpec(memory_space=pl.ANY)
    stat = (units, 1, BLOCK)
    squares = (units, HEAD_DIM, BLOCK)
    room = -(-units * (longest - 1) // GROUP) * GROUP
    near_room = -(-units * longest // GROUP) * GROUP
    weights_shape = (room, BLOCK, BLOCK)
    near_shape = (-(-units // 2 * longest // GROUP) * GROUP, BLOCK, BLOCK)
    half_stat = (units // 2, 1, BLOCK)
    half_squares = (units // 2, HEAD_DIM, BLOCK)
    params = pltpu.CompilerParams(vmem_limit_bytes=VMEM_BYTES)

    text = text_step(jnp.stack([text_keys, text_values], 0), (2,))
    keys, text = lax.optimization_barrier((video_keys, text))
    k_outer = lax.ppermute(keys, "seq", outer)
    k_inner = lax.ppermute(keys, "seq", inner)
    v_inner = lax.ppermute(video_values, "seq", inner)
    text = text_step(text, (1,))
    distance = 16
    while distance < count:
        text = text_step(text, (distance,))
        distance *= 2
    text, k_inner = lax.optimization_barrier((text, k_inner))
    item_shapes = (
        jax.ShapeDtypeStruct((near_room,), jnp.int32),
        jax.ShapeDtypeStruct((room,), jnp.int32),
        jax.ShapeDtypeStruct((4,), jnp.int32),
    )
    near_scratch = [
        pltpu.VMEM((tokens, columns // 2), jnp.bfloat16),
        pltpu.VMEM((2 * tokens, columns // 2), jnp.bfloat16),
        pltpu.VMEM((2 * tokens, columns // 2), jnp.bfloat16),
        pltpu.VMEM((columns // 2, 2 * tokens), jnp.bfloat16),
        pltpu.VMEM(near_shape, jnp.float32),
        pltpu.VMEM(near_shape, jnp.bfloat16),
        pltpu.SemaphoreType.DMA((5,)),
    ]
    near_params = dict(
        in_specs=[smem, smem] + [anywhere] * 5,
        compiler_params=params,
        cost_estimate=pl.CostEstimate(flops=1_000_000, bytes_accessed=10_000, transcendentals=0),
    )
    near_shapes = (
        jax.ShapeDtypeStruct(half_stat, jnp.float32),
        jax.ShapeDtypeStruct(half_stat, jnp.float32),
        jax.ShapeDtypeStruct(half_squares, jnp.float32),
    )
    half_values = jax.ShapeDtypeStruct((tokens, columns // 2), jnp.bfloat16)
    near_inputs = (queries, video_keys, video_values, k_inner, v_inner)
    near_items, far_items, counts, left, right, tops_a, totals_a, sums_a = pl.pallas_call(
        functools.partial(first_kernel, blocks_dev),
        out_shape=item_shapes + (half_values, half_values) + near_shapes,
        out_specs=(smem, smem, smem, anywhere, anywhere, vmem, vmem, vmem),
        scratch_shapes=near_scratch
        + [pltpu.VMEM((2, tokens, columns // 2), jnp.bfloat16), pltpu.SemaphoreType.DMA((4,))],
        name="near_first",
        **near_params,
    )(block_lists, list_lengths, *near_inputs)
    v_left = lax.ppermute(left, "seq", outer)
    tops_b, totals_b, sums_b = pl.pallas_call(
        functools.partial(near_kernel, blocks_dev, 1),
        out_shape=near_shapes,
        out_specs=(vmem, vmem, vmem),
        scratch_shapes=near_scratch,
        name="near_second",
        **near_params,
    )(near_items, counts, *near_inputs)
    parts = text_parts(text, (4, 8, 12) if count >= 16 else (4,) if count == 8 else ())
    *parts, tops_b = lax.optimization_barrier((*parts, tops_b))
    right, k_outer, *parts = lax.optimization_barrier((right, k_outer, *parts))
    v_right = lax.ppermute(right, "seq", outer)

    text_rows = text_keys.shape[0] * count
    near, weights = pl.pallas_call(
        functools.partial(middle_kernel, blocks_dev),
        out_shape=(
            jax.ShapeDtypeStruct((tokens, columns), jnp.float32),
            jax.ShapeDtypeStruct(weights_shape, jnp.bfloat16),
        ),
        in_specs=[smem, smem, vmem, vmem]
        + [anywhere] * len(parts)
        + [vmem, vmem, anywhere] * 2,
        out_specs=(vmem, anywhere),
        scratch_shapes=[
            pltpu.VMEM(stat, jnp.float32),
            pltpu.VMEM(stat, jnp.float32),
            pltpu.VMEM(stat, jnp.float32),
            pltpu.VMEM(stat, jnp.float32),
            pltpu.VMEM(stat, jnp.float32),
            pltpu.VMEM(squares, jnp.float32),
            pltpu.VMEM((units // 2, text_rows, 2 * BLOCK), jnp.bfloat16),
            pltpu.VMEM(stat, jnp.float32),
            pltpu.VMEM(stat, jnp.float32),
            pltpu.VMEM((room, 1, BLOCK), jnp.float32),
            pltpu.VMEM((room, 1, BLOCK), jnp.float32),
            pltpu.VMEM(weights_shape, jnp.float32),
            pltpu.VMEM(weights_shape, jnp.bfloat16),
            pltpu.SemaphoreType.DMA((room // GROUP,)),
            pltpu.VMEM((2, text_rows, columns), jnp.bfloat16),
            pltpu.SemaphoreType.DMA((len(parts),)),
            pltpu.VMEM((2,) + half_squares, jnp.float32),
            pltpu.SemaphoreType.DMA((2,)),
        ],
        compiler_params=params,
        cost_estimate=pl.CostEstimate(
            flops=1_000_000, bytes_accessed=10_000, transcendentals=0
        ),
        name="middle",
    )(
        far_items,
        counts,
        queries,
        k_outer,
        *parts,
        tops_a,
        totals_a,
        sums_a,
        tops_b,
        totals_b,
        sums_b,
    )

    return pl.pallas_call(
        functools.partial(last_kernel, blocks_dev),
        out_shape=jax.ShapeDtypeStruct((tokens, columns), jnp.bfloat16),
        in_specs=[smem, smem] + [anywhere] * 4,
        out_specs=vmem,
        scratch_shapes=[
            pltpu.VMEM((tokens, columns), jnp.bfloat16),
            pltpu.VMEM((tokens, columns), jnp.float32),
            pltpu.VMEM((tokens, columns), jnp.float32),
            pltpu.VMEM(weights_shape, jnp.bfloat16),
            pltpu.SemaphoreType.DMA((3,)),
            pltpu.SemaphoreType.DMA((room // GROUP,)),
        ],
        compiler_params=params,
        cost_estimate=pl.CostEstimate(
            flops=1_000_000_000, bytes_accessed=9_000_000, transcendentals=0
        ),
        name="last",
    )(far_items, counts, near, weights, v_left, v_right)


def solution(mesh):
    in_specs = (
        P(("groups", "seq"), None),
        P(("groups", "seq"), None),
        P(("groups", "seq"), None),
        P(("groups", "seq"), None),
        P(("groups", "seq"), None),
        P(None, ("groups", "seq"), None),
        P(None, ("groups", "seq")),
    )
    out_specs = P(("groups", "seq"), None)
    return jax.shard_map(
        on_device, mesh=mesh, in_specs=in_specs, out_specs=out_specs, check_vma=False
    )
```

```python
import functools
import math

import jax
import jax.numpy as jnp
from jax import lax
from jax.experimental import pallas as pl
from jax.experimental.pallas import tpu as pltpu
from jax.sharding import PartitionSpec as P

HEAD_DIM = 128
HEADS = 4
BLOCK = 128
REACH = 8
GROUP = 32
EXP2_SCALE = HEAD_DIM ** (-0.5) * math.log2(math.e)
NEVER = -1e30
NT = (((1,), (1,)), ((), ()))
VMEM_BYTES = 63 * 1024 * 1024
CODE = 64


def aligned(index):
    return pl.ds(pl.multiple_of(index * BLOCK, BLOCK), BLOCK)


def score_tile(keys, query_rows):
    return lax.dot_general(keys, query_rows, NT, preferred_element_type=jnp.float32)


def for_groups(first, count, items, blocks_dev, body):
    def step(group, carry):
        slots = []
        for slot in range(GROUP):
            position = group * GROUP + slot
            code = items[first + jnp.minimum(position, count - 1)]
            unit = code // CODE
            slots.append(
                (
                    position,
                    position < count,
                    unit,
                    unit // blocks_dev,
                    unit % blocks_dev,
                    code % CODE,
                )
            )
        body(slots)
        return carry

    lax.fori_loop(0, (count + GROUP - 1) // GROUP, step, 0)


def plan_items(blocks_dev, lists, lengths, near_items, far_items, counts):
    base = lists[0, 0, 0]
    odd = (base // blocks_dev) % 2 == 1

    def plan_unit(unit, carry):
        head = unit // blocks_dev
        local = unit % blocks_dev

        def plan_entry(entry, carry):
            near, far = carry
            block = lists[head, local, entry] - base
            is_low = block < 0
            is_high = block >= blocks_dev
            is_outer = jnp.where(odd, is_high, is_low)
            is_inner = jnp.where(odd, is_low, is_high)
            shift = jnp.where(is_low, blocks_dev, jnp.where(is_high, -blocks_dev, 0))
            code = unit * CODE + block + shift

            @pl.when(is_outer)
            def _():
                far_items[far] = code

            @pl.when(jnp.logical_not(is_outer))
            def _():
                near_items[near] = code + jnp.where(is_inner, blocks_dev, 0)

            outer = is_outer.astype(jnp.int32)
            return near + 1 - outer, far + outer

        return lax.fori_loop(0, lengths[head, local], plan_entry, carry)

    zero = jnp.int32(0)
    half = HEADS // 2 * blocks_dev
    split, far = lax.fori_loop(0, half, plan_unit, (zero, zero))
    near, far = lax.fori_loop(half, 2 * half, plan_unit, (split, far))
    counts[0] = zero
    counts[1] = split
    counts[2] = near
    counts[3] = far


def near_kernel(
    blocks_dev,
    half,
    near_items,
    counts,
    q_in,
    k_in,
    v_in,
    k_inner,
    v_inner,
    tops,
    totals,
    sums,
    q_ref,
    k_ref,
    v_ref,
    vt_ref,
    scores_all,
    weights_all,
    sems,
    prepare=None,
):
    tokens = k_in.shape[0]
    first_rows, second_rows = pl.ds(0, tokens), pl.ds(tokens, tokens)
    width = HEADS // 2 * HEAD_DIM
    lanes = pl.ds(half * width, width)
    moves = (
        (q_in.at[:, lanes], q_ref),
        (k_in.at[:, lanes], k_ref.at[first_rows]),
        (k_inner.at[:, lanes], k_ref.at[second_rows]),
        (v_in.at[:, lanes], v_ref.at[first_rows]),
        (v_inner.at[:, lanes], v_ref.at[second_rows]),
    )
    copies = [
        pltpu.make_async_copy(source, target, sems.at[index])
        for index, (source, target) in enumerate(moves)
    ]
    for copy in copies:
        copy.start()
    if prepare is not None:
        prepare()
    first = counts[half]
    count = counts[half + 1] - first

    def turn(block, carry):
        for head in range(HEADS // 2):
            lanes = slice(head * HEAD_DIM, (head + 1) * HEAD_DIM)
            vt_ref[lanes, aligned(block)] = v_ref[aligned(block), lanes].T
        return carry

    tops[...] = jnp.full(tops.shape, NEVER, jnp.float32)
    totals[...] = jnp.zeros(totals.shape, jnp.float32)
    sums[...] = jnp.zeros(sums.shape, jnp.float32)
    for copy in copies[:3]:
        copy.wait()

    def top_body(slots):
        found = []
        for position, live, unit, head, local, block in slots:
            unit, head = unit - half * HEADS // 2 * blocks_dev, head - half * HEADS // 2
            scores = score_tile(
                k_ref[aligned(block), aligned(head)], q_ref[aligned(local), aligned(head)]
            )
            scores_all[position] = scores
            found.append((unit, jnp.max(scores, axis=0, keepdims=True)))
        for unit, top in found:
            tops[unit] = jnp.maximum(tops[unit], top)

    for_groups(first, count, near_items, blocks_dev, top_body)

    def weights_body(slots):
        found = []
        for position, live, unit, head, local, block in slots:
            unit, head = unit - half * HEADS // 2 * blocks_dev, head - half * HEADS // 2
            top = jnp.where(live, tops[unit], -NEVER)
            weights = jnp.exp2((scores_all[position] - top) * EXP2_SCALE)
            weights_all[position] = weights.astype(jnp.bfloat16)
            found.append((unit, jnp.sum(weights, axis=0, keepdims=True)))
        for unit, total in found:
            totals[unit] += total

    for_groups(first, count, near_items, blocks_dev, weights_body)

    def sum_body(slots):
        found = []
        for position, live, unit, head, local, block in slots:
            unit, head = unit - half * HEADS // 2 * blocks_dev, head - half * HEADS // 2
            summed = jnp.dot(
                vt_ref[aligned(head), aligned(block)],
                weights_all[position],
                preferred_element_type=jnp.float32,
            )
            found.append((unit, summed))
        for unit, summed in found:
            sums[unit] += summed

    copies[3].wait()
    copies[4].wait()
    lax.fori_loop(0, 2 * blocks_dev, turn, 0)
    for_groups(first, count, near_items, blocks_dev, sum_body)


def first_kernel(blocks_dev, lists, lengths, *refs):
    inputs, (near_items, far_items, counts), value_halves = refs[:5], refs[5:8], refs[8:10]
    others, (held, half_sems) = refs[10:-2], refs[-2:]
    values = inputs[2]
    width = values.shape[1] // 2
    loads = [
        pltpu.make_async_copy(
            values.at[:, pl.ds(side * width, width)], held.at[side], half_sems.at[side]
        )
        for side in range(2)
    ]
    stores = [
        pltpu.make_async_copy(held.at[side], value_halves[side], half_sems.at[2 + side])
        for side in range(2)
    ]

    def prepare():
        plan_items(blocks_dev, lists, lengths, near_items, far_items, counts)
        for load, store in zip(loads, stores):
            load.wait()
            store.start()

    for load in loads:
        load.start()
    near_kernel(blocks_dev, 0, near_items, counts, *inputs, *others, prepare=prepare)
    for store in stores:
        store.wait()


def middle_kernel(
    blocks_dev,
    far_items,
    counts,
    q_ref,
    k_far,
    *refs,
):
    parts, refs = refs[:-26], refs[-26:]
    (
        tops_a,
        totals_a,
        sums_a,
        tops_b,
        totals_b,
        sums_b,
        near_out,
        weights_out,
        tops,
        totals,
        levels,
        text_tops,
        text_totals,
        text_sums,
        text_weights,
        near_tops,
        near_totals,
        item_tops,
        item_totals,
        scores_all,
        weights_all,
        out_sems,
        text,
        text_sems,
        sums_all,
        sums_sems,
    ) = refs
    rows = parts[0].shape[1]
    copies = [
        pltpu.make_async_copy(
            part, text.at[:, pl.ds(index * rows, rows)], text_sems.at[index]
        )
        for index, part in enumerate(parts)
    ]
    sums_copies = [
        pltpu.make_async_copy(source, sums_all.at[side], sums_sems.at[side])
        for side, source in enumerate((sums_a, sums_b))
    ]
    for copy in copies + sums_copies:
        copy.start()
    half = HEADS // 2 * blocks_dev
    near_tops[:half] = tops_a[...]
    near_tops[half:] = tops_b[...]
    near_totals[:half] = totals_a[...]
    near_totals[half:] = totals_b[...]
    tops[...] = near_tops[...]
    count = counts[3]

    def total_body(slots):
        found = []
        for position, live, unit, head, local, block in slots:
            scores = score_tile(
                k_far[aligned(block), aligned(head)], q_ref[aligned(local), aligned(head)]
            )
            top = jnp.max(scores, axis=0, keepdims=True)
            total = jnp.sum(jnp.exp2((scores - top) * EXP2_SCALE), axis=0, keepdims=True)
            scores_all[position] = scores
            found.append((unit, position, jnp.where(live, top, NEVER), total))
        for unit, position, top, total in found:
            item_tops[position] = top
            item_totals[position] = total
            tops[unit] = jnp.maximum(tops[unit], top)

    for_groups(0, count, far_items, blocks_dev, total_body)
    for copy in copies:
        copy.wait()
    pairs = blocks_dev // 2

    def text_weights_head(head, carry):
        keys = text[0, :, aligned(head)]
        for pair in range(pairs):
            rows = pl.ds(pair * 2 * BLOCK, 2 * BLOCK)
            scores = score_tile(keys, q_ref[rows, aligned(head)])
            top = jnp.max(scores, axis=0, keepdims=True)
            weights = jnp.exp2((scores - top) * EXP2_SCALE)
            text_weights[head * pairs + pair] = weights.astype(jnp.bfloat16)
            total = jnp.sum(weights, axis=0, keepdims=True)
            for side in range(2):
                unit = head * blocks_dev + pair * 2 + side
                lanes = slice(side * BLOCK, (side + 1) * BLOCK)
                text_tops[unit] = top[:, lanes]
                text_totals[unit] = total[:, lanes]
        return carry

    lax.fori_loop(0, HEADS, text_weights_head, 0)

    def text_sums_head(head, carry):
        values_t = text[1, :, aligned(head)].T
        for pair in range(pairs):
            summed = jnp.dot(
                values_t, text_weights[head * pairs + pair], preferred_element_type=jnp.float32
            )
            for side in range(2):
                unit = head * blocks_dev + pair * 2 + side
                text_sums[unit] = summed[:, side * BLOCK : (side + 1) * BLOCK]
        return carry

    lax.fori_loop(0, HEADS, text_sums_head, 0)
    tops[...] = jnp.maximum(tops[...], text_tops[...])
    near_share = near_totals[...] * jnp.exp2((near_tops[...] - tops[...]) * EXP2_SCALE)
    text_share = text_totals[...] * jnp.exp2((text_tops[...] - tops[...]) * EXP2_SCALE)
    totals[...] = near_share + text_share

    def fold_body(slots):
        found = []
        for position, live, unit, head, local, block in slots:
            add = jnp.exp2((item_tops[position] - tops[unit]) * EXP2_SCALE)
            found.append((unit, item_totals[position] * add))
        for unit, total in found:
            totals[unit] += total

    for_groups(0, count, far_items, blocks_dev, fold_body)
    levels[...] = tops[...] * EXP2_SCALE + jnp.log2(totals[...])

    def weights_body(slots):
        for position, live, unit, head, local, block in slots:
            level = jnp.where(live, levels[unit], -NEVER)
            weights = jnp.exp2(scores_all[position] * EXP2_SCALE - level).astype(jnp.bfloat16)
            weights_all[position] = weights.T
        first = pl.multiple_of(slots[0][0], GROUP)
        part = pl.ds(first, GROUP)
        pltpu.make_async_copy(
            weights_all.at[part], weights_out.at[part], out_sems.at[first // GROUP]
        ).start()

    for_groups(0, count, far_items, blocks_dev, weights_body)

    for copy in sums_copies:
        copy.wait()

    def near_rows(local, carry):
        for head in range(HEADS):
            unit = head * blocks_dev + local
            sums = sums_all.at[head // (HEADS // 2)]
            near_factor = jnp.exp2(near_tops[unit] * EXP2_SCALE - levels[unit])
            text_factor = jnp.exp2(text_tops[unit] * EXP2_SCALE - levels[unit])
            near_out[aligned(local), head * HEAD_DIM : (head + 1) * HEAD_DIM] = (
                sums[head % (HEADS // 2) * blocks_dev + local] * near_factor
                + text_sums[unit] * text_factor
            ).T
        return carry

    lax.fori_loop(0, blocks_dev, near_rows, 0)

    def settle(group, carry):
        part = pl.ds(pl.multiple_of(group * GROUP, GROUP), GROUP)
        pltpu.make_async_copy(weights_all.at[part], weights_out.at[part], out_sems.at[group]).wait()
        return carry

    lax.fori_loop(0, (count + GROUP - 1) // GROUP, settle, 0)


def last_kernel(
    blocks_dev,
    far_items,
    counts,
    near,
    weights,
    v_left,
    v_right,
    out_ref,
    v_far,
    near_rows,
    total_rows,
    weights_all,
    sems,
    weight_sems,
):
    count = counts[3]
    groups = (count + GROUP - 1) // GROUP

    def weight_copy(group):
        part = pl.ds(pl.multiple_of(group * GROUP, GROUP), GROUP)
        return pltpu.make_async_copy(weights.at[part], weights_all.at[part], weight_sems.at[group])

    width = v_left.shape[1]
    values_copies = [
        pltpu.make_async_copy(half, v_far.at[:, pl.ds(side * width, width)], sems.at[side])
        for side, half in enumerate((v_left, v_right))
    ]
    near_copy = pltpu.make_async_copy(near, near_rows, sems.at[2])
    for copy in values_copies:
        copy.start()

    def begin(group, carry):
        weight_copy(group).start()
        return carry

    lax.fori_loop(0, groups, begin, 0)
    near_copy.start()
    total_rows[...] = jnp.zeros(total_rows.shape, jnp.float32)
    for copy in values_copies:
        copy.wait()

    def body(slots):
        weight_copy(slots[0][0] // GROUP).wait()
        parts = []
        for position, live, unit, head, local, block in slots:
            parts.append(
                jnp.dot(
                    weights_all[position],
                    v_far[aligned(block), aligned(head)],
                    preferred_element_type=jnp.float32,
                )
            )
        for slot, part in zip(slots, parts):
            total_rows[aligned(slot[4]), aligned(slot[3])] += part

    for_groups(0, count, far_items, blocks_dev, body)
    near_copy.wait()
    out_ref[...] = (total_rows[...] + near_rows[...]).astype(jnp.bfloat16)


def text_parts(text, distances):
    count = lax.axis_size("seq")
    parts = [text]
    for distance in distances:
        parts.append(lax.ppermute(text, "seq", [(i, i ^ distance) for i in range(count)]))
    return parts


def text_step(text, distances):
    return jnp.concatenate(text_parts(text, distances), axis=1)


def on_device(queries, video_keys, video_values, text_keys, text_values, block_lists, list_lengths):
    tokens = queries.shape[0]
    columns = queries.shape[1]
    blocks_dev = tokens // BLOCK
    count = lax.axis_size("seq")
    assert blocks_dev == REACH and 2 * blocks_dev <= CODE and count & (count - 1) == 0
    units = HEADS * blocks_dev
    longest = block_lists.shape[2]
    inner = [(i, i ^ 1) for i in range(count)]
    outer = [(i, i + 1) for i in range(1, count - 1, 2)]
    outer += [(target, source) for source, target in outer]

    smem = pl.BlockSpec(memory_space=pltpu.SMEM)
    vmem = pl.BlockSpec(memory_space=pltpu.VMEM)
    anywhere = pl.BlockSpec(memory_space=pl.ANY)
    stat = (units, 1, BLOCK)
    squares = (units, HEAD_DIM, BLOCK)
    room = -(-units * (longest - 1) // GROUP) * GROUP
    near_room = -(-units * longest // GROUP) * GROUP
    weights_shape = (room, BLOCK, BLOCK)
    near_shape = (-(-units // 2 * longest // GROUP) * GROUP, BLOCK, BLOCK)
    half_stat = (units // 2, 1, BLOCK)
    half_squares = (units // 2, HEAD_DIM, BLOCK)
    params = pltpu.CompilerParams(vmem_limit_bytes=VMEM_BYTES)

    text = text_step(jnp.stack([text_keys, text_values], 0), (2,))
    keys, text = lax.optimization_barrier((video_keys, text))
    k_outer = lax.ppermute(keys, "seq", outer)
    k_inner = lax.ppermute(keys, "seq", inner)
    v_inner = lax.ppermute(video_values, "seq", inner)
    text = text_step(text, (1,))
    distance = 16
    while distance < count:
        text = text_step(text, (distance,))
        distance *= 2
    text, k_inner = lax.optimization_barrier((text, k_inner))
    item_shapes = (
        jax.ShapeDtypeStruct((near_room,), jnp.int32),
        jax.ShapeDtypeStruct((room,), jnp.int32),
        jax.ShapeDtypeStruct((4,), jnp.int32),
    )
    near_scratch = [
        pltpu.VMEM((tokens, columns // 2), jnp.bfloat16),
        pltpu.VMEM((2 * tokens, columns // 2), jnp.bfloat16),
        pltpu.VMEM((2 * tokens, columns // 2), jnp.bfloat16),
        pltpu.VMEM((columns // 2, 2 * tokens), jnp.bfloat16),
        pltpu.VMEM(near_shape, jnp.float32),
        pltpu.VMEM(near_shape, jnp.bfloat16),
        pltpu.SemaphoreType.DMA((5,)),
    ]
    near_params = dict(
        in_specs=[smem, smem] + [anywhere] * 5,
        compiler_params=params,
        cost_estimate=pl.CostEstimate(flops=1_000_000, bytes_accessed=10_000, transcendentals=0),
    )
    near_shapes = (
        jax.ShapeDtypeStruct(half_stat, jnp.float32),
        jax.ShapeDtypeStruct(half_stat, jnp.float32),
        jax.ShapeDtypeStruct(half_squares, jnp.float32),
    )
    half_values = jax.ShapeDtypeStruct((tokens, columns // 2), jnp.bfloat16)
    near_inputs = (queries, video_keys, video_values, k_inner, v_inner)
    near_items, far_items, counts, left, right, tops_a, totals_a, sums_a = pl.pallas_call(
        functools.partial(first_kernel, blocks_dev),
        out_shape=item_shapes + (half_values, half_values) + near_shapes,
        out_specs=(smem, smem, smem, anywhere, anywhere, vmem, vmem, vmem),
        scratch_shapes=near_scratch
        + [pltpu.VMEM((2, tokens, columns // 2), jnp.bfloat16), pltpu.SemaphoreType.DMA((4,))],
        name="near_first",
        **near_params,
    )(block_lists, list_lengths, *near_inputs)
    v_left = lax.ppermute(left, "seq", outer)
    tops_b, totals_b, sums_b = pl.pallas_call(
        functools.partial(near_kernel, blocks_dev, 1),
        out_shape=near_shapes,
        out_specs=(vmem, vmem, vmem),
        scratch_shapes=near_scratch,
        name="near_second",
        **near_params,
    )(near_items, counts, *near_inputs)
    parts = text_parts(text, (4, 8, 12) if count >= 16 else (4,) if count == 8 else ())
    *parts, tops_b = lax.optimization_barrier((*parts, tops_b))
    right, k_outer, *parts = lax.optimization_barrier((right, k_outer, *parts))
    v_right = lax.ppermute(right, "seq", outer)

    text_rows = text_keys.shape[0] * count
    near, weights = pl.pallas_call(
        functools.partial(middle_kernel, blocks_dev),
        out_shape=(
            jax.ShapeDtypeStruct((tokens, columns), jnp.float32),
            jax.ShapeDtypeStruct(weights_shape, jnp.bfloat16),
        ),
        in_specs=[smem, smem, vmem, vmem]
        + [anywhere] * len(parts)
        + [vmem, vmem, anywhere] * 2,
        out_specs=(vmem, anywhere),
        scratch_shapes=[
            pltpu.VMEM(stat, jnp.float32),
            pltpu.VMEM(stat, jnp.float32),
            pltpu.VMEM(stat, jnp.float32),
            pltpu.VMEM(stat, jnp.float32),
            pltpu.VMEM(stat, jnp.float32),
            pltpu.VMEM(squares, jnp.float32),
            pltpu.VMEM((units // 2, text_rows, 2 * BLOCK), jnp.bfloat16),
            pltpu.VMEM(stat, jnp.float32),
            pltpu.VMEM(stat, jnp.float32),
            pltpu.VMEM((room, 1, BLOCK), jnp.float32),
            pltpu.VMEM((room, 1, BLOCK), jnp.float32),
            pltpu.VMEM(weights_shape, jnp.float32),
            pltpu.VMEM(weights_shape, jnp.bfloat16),
            pltpu.SemaphoreType.DMA((room // GROUP,)),
            pltpu.VMEM((2, text_rows, columns), jnp.bfloat16),
            pltpu.SemaphoreType.DMA((len(parts),)),
            pltpu.VMEM((2,) + half_squares, jnp.float32),
            pltpu.SemaphoreType.DMA((2,)),
        ],
        compiler_params=params,
        cost_estimate=pl.CostEstimate(
            flops=1_000_000, bytes_accessed=10_000, transcendentals=0
        ),
        name="middle",
    )(
        far_items,
        counts,
        queries,
        k_outer,
        *parts,
        tops_a,
        totals_a,
        sums_a,
        tops_b,
        totals_b,
        sums_b,
    )

    return pl.pallas_call(
        functools.partial(last_kernel, blocks_dev),
        out_shape=jax.ShapeDtypeStruct((tokens, columns), jnp.bfloat16),
        in_specs=[smem, smem] + [anywhere] * 4,
        out_specs=vmem,
        scratch_shapes=[
            pltpu.VMEM((tokens, columns), jnp.bfloat16),
            pltpu.VMEM((tokens, columns), jnp.float32),
            pltpu.VMEM((tokens, columns), jnp.float32),
            pltpu.VMEM(weights_shape, jnp.bfloat16),
            pltpu.SemaphoreType.DMA((3,)),
            pltpu.SemaphoreType.DMA((room // GROUP,)),
        ],
        compiler_params=params,
        cost_estimate=pl.CostEstimate(
            flops=1_000_000_000, bytes_accessed=9_000_000, transcendentals=0
        ),
        name="last",
    )(far_items, counts, near, weights, v_left, v_right)


def solution(mesh):
    in_specs = (
        P(("groups", "seq"), None),
        P(("groups", "seq"), None),
        P(("groups", "seq"), None),
        P(("groups", "seq"), None),
        P(("groups", "seq"), None),
        P(None, ("groups", "seq"), None),
        P(None, ("groups", "seq")),
    )
    out_specs = P(("groups", "seq"), None)
    return jax.shard_map(
        on_device, mesh=mesh, in_specs=in_specs, out_specs=out_specs, check_vma=False
    )
```
